256 devices in a mesh: seg: 8 (over z_lo, core), slab: 32 (over z_hi, y, x).
Axes of the slice: x: 4, y: 4, z: 8 (z_hi: 2, z_lo: 4; z = z_hi * 4 + z_lo), core: 2. Of those that a mesh axis runs over, the one named last changes fastest.
Arguments:
- activity: float32 [2048, 2048], P('slab'), may hold values from 0.5 to 1.5
- measured: float32 [32, 8, 64, 32, 384], P('seg', None, 'slab'), may hold values from 0.5 to 4
- randoms: int32 [32, 8, 2048, 384], P('seg', None, 'slab'), may hold values from 0 to 8
- footprint: bfloat16 [8, 2048, 384], replicated, may hold values from 0 to 577, as said below
- kernel: float32 [16, 9], replicated, may hold values from 0.03 to 0.3
- dead_counts: int32 [65536], replicated, may hold values from 0 to 1000
- crystals: int32 [2, 8, 384], replicated, may hold values from 0 to 65535
- sensitivity: float32 [2048, 2048], P('slab'), may hold values from 30 to 120
Outputs:
- new_activity: float32 [2048, 2048], P('slab')
The draws below stay inside these ranges and needn't reach their ends.
Inputs may be any that keep to these rules, and one draw needn't show every extreme that they name: footprint weights are non-negative.
All inputs are finite; a program needn't handle non-finite values.
Results may differ from the reference program's by a relative error of at most 0.0003.
Values sent between devices are 32-bit elements; how exact they have to be, the bound alone decides.
No kernel may reach another device: no remote copies, remote signals or barrier semaphores. Data moves between devices by JAX's collectives and lax.ppermute only.
A program may use at most 128 MiB of HBM per device.

```python
import math
import jax
import jax.numpy as jnp
from jax import lax

PIX = 2048
BINS = 384
VIEWS = 8
HALO = 4
TAPS = 9
SEGS = 32
HALF = 16
Z_DEV = 64
NZ = 2048
CRYS = 65536
N_SLAB = 32


def draw_footprint(key, part):
    key = jax.random.fold_in(key, 7)
    order_key = jax.random.fold_in(key, 1)
    level_key = jax.random.fold_in(key, 2)
    floor_key = jax.random.fold_in(key, 3)
    view_keys = jax.random.split(order_key, VIEWS)
    orders = jax.vmap(lambda single: jax.random.permutation(single, PIX))(view_keys)
    owner = orders.astype(jnp.int32) * BINS // PIX
    band = owner[:, :, None] == jnp.arange(BINS, dtype=jnp.int32)[None, None, :]
    level = jax.random.uniform(level_key, (VIEWS, PIX, BINS), jnp.float32, 0.5, 1.5) * BINS
    floor = jax.random.uniform(floor_key, (VIEWS, PIX, BINS), jnp.float32, 0.0, 0.2)
    return jnp.where(band, level, floor).astype(jnp.bfloat16)


def set_ends(array, rng, smallest, high):
    longest = array.shape.index(max(array.shape))
    spots = []
    for shift in (0, 1):
        where = [jax.random.randint(jax.random.fold_in(rng, axis), (), 0, length) for axis, length in enumerate(array.shape)]
        where[longest] = (where[longest] + shift) % array.shape[longest]
        spots.append(tuple(where))
    return array.at[spots[0]].set(smallest).at[spots[1]].set(high)


def block_scale(rng, extent, cuts, least, largest):
    def one(dim, shards_of):
        heights = jax.random.uniform(jax.random.fold_in(jax.random.fold_in(rng, 6), dim), (shards_of,), jnp.float32, least / len(cuts), largest / len(cuts))
        return jnp.repeat(jnp.exp(heights), extent[dim] // shards_of).reshape((-1,) + (1,) * (len(extent) - dim - 1))

    factor_of = one(*cuts[0])
    for cut in cuts[1:]:
        factor_of = factor_of * one(*cut)
    return factor_of


def setup_inputs(seed: int = 0) -> dict:
    seeds = jax.random.split(jax.random.key(seed), 9)
    activity = jnp.clip(0.5 + 1.0 * jax.random.uniform(seeds[0], (NZ, PIX), jnp.float32) ** block_scale(seeds[0], (NZ, PIX), ((0, 32),), -0.2, 0.2), 0.5, 1.5)
    measured = jnp.clip(jnp.exp(math.log(4.0) - 2.0794415 * jax.random.uniform(seeds[1], (SEGS, VIEWS, Z_DEV, N_SLAB, BINS), jnp.float32) ** block_scale(seeds[1], (SEGS, VIEWS, Z_DEV, N_SLAB, BINS), ((0, 8), (2, 32)), -0.2, 0.2)), 0.5, 4.0)
    randoms = set_ends(jax.random.randint(seeds[2], (SEGS, VIEWS, NZ, BINS), 0, 9), jax.random.fold_in(seeds[2], 1), 0, 8).astype(jnp.int32)
    footprint = draw_footprint(jax.random.fold_in(seeds[8], 71), 0)
    kernel = jnp.clip(jnp.exp(jax.random.uniform(seeds[4], (HALF, TAPS), jnp.float32, math.log(0.03), math.log(0.3))), 0.03, 0.3)
    dead_counts = set_ends(jax.random.randint(seeds[5], (CRYS,), 0, 1001), jax.random.fold_in(seeds[5], 1), 0, 1000).astype(jnp.int32)
    crystals = set_ends(jax.random.randint(seeds[6], (2, VIEWS, BINS), 0, CRYS), jax.random.fold_in(seeds[6], 1), 0, CRYS - 1).astype(jnp.int32)
    sensitivity = jnp.clip(jnp.exp(math.log(120.0) - 1.3862944 * jax.random.uniform(seeds[7], (NZ, PIX), jnp.float32) ** block_scale(seeds[7], (NZ, PIX), ((0, 32),), -0.2, 0.2)), 30.0, 120.0)
    return dict(activity=activity, measured=measured, randoms=randoms, footprint=footprint, kernel=kernel, dead_counts=dead_counts, crystals=crystals, sensitivity=sensitivity)


dead_time_tau = 0.001


def reference(activity, measured, randoms, footprint, kernel, dead_counts, crystals, sensitivity):
    kernels = jnp.concatenate([kernel, kernel[:, ::-1]], axis=0)
    counts = dead_counts[crystals].astype(jnp.float32)
    efficiency = 1.0 / ((1.0 + dead_time_tau * counts[0]) * (1.0 + dead_time_tau * counts[1]))
    rows = jnp.transpose(measured, (0, 1, 3, 2, 4)).reshape(SEGS, VIEWS, NZ, BINS)
    foot_wide = footprint.astype(jnp.float32)
    padded = jnp.pad(activity, ((HALO, HALO), (0, 0)))
    tap_count = 2 * HALO + 1

    def segment_step(running, pieces):
        weights, measured_rows, random_rows = pieces
        axial_rows = jnp.zeros((NZ, PIX), jnp.float32)
        for offset in range(tap_count):
            axial_rows = axial_rows + weights[offset] * padded[offset:offset + NZ]
        axial_rows = axial_rows.astype(jnp.bfloat16)
        projected = jnp.einsum("zp,vpb->vzb", axial_rows.astype(jnp.float32), foot_wide) / PIX
        expected = efficiency[:, None, :] * projected + 0.25 * (random_rows.astype(jnp.float32) + 1.0)
        weighted = (efficiency[:, None, :] * measured_rows / expected).astype(jnp.bfloat16)
        spread = jnp.einsum("vzb,vpb->zp", weighted.astype(jnp.float32), foot_wide) / PIX
        spread_pad = jnp.pad(spread, ((HALO, HALO), (0, 0)))
        for offset in range(tap_count):
            start = 2 * HALO - offset
            running = running + weights[offset] * spread_pad[start:start + NZ]
        return running, None

    summed, _ = lax.scan(segment_step, jnp.zeros((NZ, PIX), jnp.float32), (kernels, rows, randoms))
    return activity * summed / sensitivity
```

```python
import functools
import jax
import jax.numpy as jnp
from jax import lax
from jax.experimental import pallas as pl
from jax.experimental.pallas import tpu as pltpu
from jax.sharding import PartitionSpec as P

dead_time_tau = 0.001
f32 = jnp.float32
bf16 = jnp.bfloat16
LANES = 128
VMEM = pl.BlockSpec(memory_space=pltpu.VMEM)
SMEM = pl.BlockSpec(memory_space=pltpu.SMEM)


def params(mib):
    return pltpu.CompilerParams(vmem_limit_bytes=mib << 20)


def lane_blocks(bins):
    return bins // LANES


def relay_kernel(*refs):
    *m_refs, o_ref = refs
    segs, _, inner, slabs, _ = m_refs[0].shape
    rows = segs * inner

    for lane, m_ref in enumerate(m_refs):
        flat = m_ref.reshape(rows * slabs, LANES)
        for s in range(slabs):
            o_ref[s, 0, :, lane * LANES : (lane + 1) * LANES] = flat[pl.ds(s, rows, stride=slabs), :]


def relay(measured):
    segs, views, inner, slabs, bins = measured.shape
    rows = segs * inner
    lanes = [
        pl.BlockSpec((segs, 1, inner, slabs, LANES), lambda v, lane=lane: (0, v, 0, 0, lane))
        for lane in range(lane_blocks(bins))
    ]
    return pl.pallas_call(
        relay_kernel,
        grid=(views,),
        in_specs=lanes,
        out_specs=pl.BlockSpec((slabs, 1, rows, bins), lambda v: (0, v, 0, 0)),
        out_shape=jax.ShapeDtypeStruct((slabs, views, rows, bins), f32),
        compiler_params=params(16),
    )(*[measured] * len(lanes))


def split_two(x):
    hi = x.astype(bf16)
    return hi, (x - hi.astype(f32)).astype(bf16)


def efficiency_kernel(t_ref, c_ref, o_ref):
    lanes, depth = t_ref.shape
    views = o_ref.shape[0]
    bins = c_ref.shape[-1]
    table = t_ref[...].astype(f32)
    first = table.astype(bf16)
    rest = table - first.astype(f32)
    second = rest.astype(bf16)
    third = (rest - second.astype(f32)).astype(bf16)
    pieces = jnp.concatenate([first, second, third], axis=0)
    depth_ids = lax.broadcasted_iota(jnp.int32, (depth, bins), 0)
    lane_ids = lax.broadcasted_iota(jnp.int32, (lanes, bins), 0)

    def look(index):
        row = index // lanes
        hot = jnp.where(depth_ids == row, 1.0, 0.0).astype(bf16)
        got = jnp.dot(pieces, hot, preferred_element_type=f32)
        value = got[:lanes] + got[lanes : 2 * lanes] + got[2 * lanes :]
        return jnp.sum(jnp.where(lane_ids == index - row * lanes, value, 0.0), axis=0, keepdims=True)

    def one_view(v, carry):
        first_factor = 1.0 + dead_time_tau * look(c_ref[0, v])
        second_factor = 1.0 + dead_time_tau * look(c_ref[1, v])
        o_ref[v] = 1.0 / (first_factor * second_factor)
        return carry

    lax.fori_loop(0, views, one_view, 0)


def efficiency_of(dead_counts, crystals):
    _, views, bins = crystals.shape
    table = dead_counts.reshape(-1, 128).T
    return pl.pallas_call(
        efficiency_kernel,
        in_specs=[VMEM, VMEM],
        out_specs=VMEM,
        out_shape=jax.ShapeDtypeStruct((views, 1, bins), f32),
        compiler_params=params(16),
    )(table, crystals.reshape(2, views, 1, bins))


def forward_kernel(op_ref, ext_ref, foot_ref, eff_ref, *refs):
    lanes = len(refs) // 2 - 1
    rand_refs, o_ref, rows_ref, order_refs = refs[:lanes], refs[lanes], refs[lanes + 1], refs[lanes + 2 :]
    segs, _, slices, _ = rand_refs[0].shape
    pixels = ext_ref.shape[1]
    inner = 2
    count = slices // inner

    @pl.when(pl.program_id(0) == 0)
    def _():
        rows_ref[...] = jnp.dot(
            op_ref[...], ext_ref[...], preferred_element_type=f32, precision=lax.Precision.HIGHEST
        ).astype(bf16)

    projected = jnp.dot(rows_ref[...], foot_ref[0], preferred_element_type=f32) * (1.0 / pixels)
    for lane in range(lanes):
        flat = rand_refs[lane].reshape(segs * slices, LANES)
        order_ref = order_refs[lane]
        for g in range(segs):
            for a in range(inner):
                got = flat[pl.ds(g * slices + a, count, stride=inner), :].astype(f32)
                order_ref[pl.ds(g * inner + a, count, stride=segs * inner), :] = 0.25 * (got + 1.0)
        cols = slice(lane * LANES, (lane + 1) * LANES)
        eff = eff_ref[0, :, cols]
        o_ref[0, :, cols] = eff / (eff * projected[:, cols] + order_ref[...])


def forward(operator, extended, footprint, randoms, efficiency):
    segs, views, slices, bins = randoms.shape
    pixels = footprint.shape[1]
    rows = segs * slices
    lanes = [
        pl.BlockSpec((segs, 1, slices, LANES), lambda v, lane=lane: (0, v, 0, lane))
        for lane in range(lane_blocks(bins))
    ]
    return pl.pallas_call(
        forward_kernel,
        grid=(views,),
        in_specs=[
            VMEM,
            VMEM,
            pl.BlockSpec((1, pixels, bins), lambda v: (v, 0, 0)),
            pl.BlockSpec((1, 1, bins), lambda v: (v, 0, 0)),
        ]
        + lanes,
        out_specs=pl.BlockSpec((1, rows, bins), lambda v: (v, 0, 0)),
        out_shape=jax.ShapeDtypeStruct((views, rows, bins), f32),
        scratch_shapes=[pltpu.VMEM((rows, pixels), bf16)] + [pltpu.VMEM((rows, LANES), f32)] * len(lanes),
        compiler_params=params(32),
        cost_estimate=pl.CostEstimate(
            flops=2 * rows * pixels * bins * views, bytes_accessed=20 << 20, transcendentals=0
        ),
    )(operator, extended, footprint, efficiency, *[randoms] * len(lanes))


def back_kernel(me_ref, opt_ref, x_ref, factor_ref, foot_ref, *refs):
    mine_refs, other_ref = refs[:4], refs[4]
    split_ref, acc_ref = refs[5], refs[6]
    ext = opt_ref.shape[0]
    pixels = acc_ref.shape[1]
    step = pl.program_id(0)
    rows = factor_ref.shape[1]

    @pl.when(step == 0)
    def _():
        hi, lo = split_two(opt_ref[...])
        split_ref[:ext] = hi
        split_ref[ext:] = lo
        acc_ref[...] = jnp.zeros_like(acc_ref)

    weighted = (factor_ref[0] * x_ref[:, 0].reshape(rows, -1)).astype(bf16)
    both = jnp.dot(split_ref[...], weighted, preferred_element_type=f32)
    hi, lo = split_two(both[:ext] + both[ext:])
    spread = lax.dot_general(
        jnp.concatenate([hi, lo], axis=0), foot_ref[0], (((1,), (1,)), ((), ())), preferred_element_type=f32
    )
    acc_ref[...] += spread[:ext] + spread[ext:]

    @pl.when(step == pl.num_programs(0) - 1)
    def _():
        kept, width = mine_refs[0].shape
        for k in range(4):
            for c in range(2):
                block = me_ref[0] ^ (2 * k + c)
                part = acc_ref[:kept, pl.ds(pl.multiple_of(block * width, width), width)] * (1.0 / pixels)
                if c == 0:
                    mine_refs[k][...] = part
                else:
                    other_ref[k] = part


def back(me, operator_t, rows_in, factor, footprint, kept):
    views, rows, bins = factor.shape
    slabs, _, inner, _ = rows_in.shape
    pixels = footprint.shape[1]
    width = pixels // 8
    ext = operator_t.shape[0]
    return pl.pallas_call(
        back_kernel,
        grid=(views,),
        in_specs=[
            SMEM,
            VMEM,
            pl.BlockSpec((slabs, 1, inner, bins), lambda v: (0, v, 0, 0)),
            pl.BlockSpec((1, rows, bins), lambda v: (v, 0, 0)),
            pl.BlockSpec((1, pixels, bins), lambda v: (v, 0, 0)),
        ],
        out_specs=[VMEM] * 5,
        out_shape=[jax.ShapeDtypeStruct((kept, width), f32)] * 4
        + [jax.ShapeDtypeStruct((4, kept, width), f32)],
        scratch_shapes=[pltpu.VMEM((2 * ext, rows), bf16), pltpu.VMEM((ext, pixels), f32)],
        compiler_params=params(32),
        cost_estimate=pl.CostEstimate(
            flops=4 * ext * pixels * bins * views, bytes_accessed=20 << 20, transcendentals=0
        ),
    )(me, operator_t, rows_in, factor, footprint)


def assemble_kernel(me_ref, *refs):
    near_refs, far_ref, o_ref = refs[:4], refs[4], refs[5]
    width = near_refs[0].shape[1]
    for k in range(4):
        for c in range(2):
            block = me_ref[0] ^ (2 * k + c)
            part = near_refs[k][...] if c == 0 else far_ref[k]
            o_ref[:, pl.ds(pl.multiple_of(block * width, width), width)] = part


def assemble(me, near, far):
    slices, width = near[0].shape
    return pl.pallas_call(
        assemble_kernel,
        in_specs=[SMEM] + [VMEM] * 5,
        out_specs=VMEM,
        out_shape=jax.ShapeDtypeStruct((slices, width * 8), f32),
        compiler_params=params(16),
    )(me, *near, far)


def local(activity, measured, randoms, footprint, kernel, dead_counts, crystals, sensitivity):
    segs, views, inner, slabs, bins = measured.shape
    slices, pixels = activity.shape
    taps = kernel.shape[1]
    margin = (taps - 1) // 2
    width = pixels // 8
    group = lax.axis_index("seg")
    me = group.astype(jnp.int32).reshape(1)
    halves = lax.axis_size("seg") // 2

    def swap(x, k):
        return lax.ppermute(x, "seg", [(i, i ^ k) for i in range(2 * halves)])

    def shift(x, up):
        pairs = [(i + 1, i) if up else (i, i + 1) for i in range(slabs - 1)]
        return lax.ppermute(x, "slab", pairs)

    rows_out = relay(measured)
    rows_in = lax.all_to_all(rows_out, "slab", split_axis=0, concat_axis=0, tiled=True)

    plain = lax.dynamic_slice_in_dim(kernel, group % halves * segs, segs, 0)
    weights = jnp.where(group >= halves, plain[:, ::-1], plain)
    ext = slices + 2 * margin
    ext_pad = ext + 8
    tap = jnp.arange(ext_pad)[None, None, None, :] - (
        inner * jnp.arange(slabs)[:, None, None, None] + jnp.arange(inner)[None, None, :, None]
    )
    operator = jnp.zeros((slabs, segs, inner, ext_pad), f32)
    for k in range(taps):
        operator = operator + jnp.where(tap == k, weights[None, :, k, None, None], 0.0)
    operator = operator.reshape(slabs * segs * inner, ext_pad)

    extended = jnp.concatenate(
        [
            shift(activity[slices - margin :], False),
            activity,
            shift(activity[:margin], True),
            jnp.zeros((ext_pad - ext, pixels), f32),
        ],
        axis=0,
    )
    efficiency = efficiency_of(dead_counts, crystals)
    factor = forward(operator, extended, footprint, randoms, efficiency)

    *mine, other = back(me, operator.T, rows_in, factor, footprint, ext)
    theirs = swap(other, 1)
    pair = [mine[k] + theirs[k] for k in range(4)]
    total = pair[0]
    for k in range(1, 4):
        total = total + swap(pair[k], 2 * k)
    above = shift(total[ext - margin :], False)
    below = shift(total[:margin], True)
    summed = jnp.concatenate(
        [
            total[margin : 2 * margin] + above,
            total[2 * margin : slices],
            total[slices : slices + margin] + below,
        ],
        axis=0,
    )
    start = group * width
    ratio = lax.dynamic_slice_in_dim(activity, start, width, 1) / lax.dynamic_slice_in_dim(
        sensitivity, start, width, 1
    )
    block = summed * ratio
    near = [block] + [swap(block, 2 * k) for k in range(1, 4)]
    far = swap(jnp.stack(near), 1)
    return assemble(me, near, far)


def solution(mesh):
    placed = (
        P("slab", None),
        P("seg", None, "slab", None, None),
        P("seg", None, "slab", None),
        P(),
        P(),
        P(),
        P(),
        P("slab", None),
    )
    return jax.shard_map(
        local, mesh=mesh, in_specs=placed, out_specs=P("slab", None), check_vma=False
    )
```

```python
import functools
import jax
import jax.numpy as jnp
from jax import lax
from jax.experimental import pallas as pl
from jax.experimental.pallas import tpu as pltpu
from jax.sharding import PartitionSpec as P

dead_time_tau = 0.001
f32 = jnp.float32
bf16 = jnp.bfloat16
LANES = 128
VMEM = pl.BlockSpec(memory_space=pltpu.VMEM)
SMEM = pl.BlockSpec(memory_space=pltpu.SMEM)
HBM = pl.BlockSpec(memory_space=pltpu.HBM)
SMALL = pl.CostEstimate(flops=1, bytes_accessed=1, transcendentals=0)
LARGE = pl.CostEstimate(flops=10**12, bytes_accessed=1 << 20, transcendentals=0)


def params(mib):
    return pltpu.CompilerParams(vmem_limit_bytes=mib << 20)


def lane_blocks(bins):
    return bins // LANES


def relay_kernel(sides, lanes, half_ref, *refs):
    m_refs, o_ref = refs[:lanes], refs[-1]
    segs, _, inner, slabs, _ = m_refs[0].shape
    rows = segs * inner
    count = o_ref.shape[0]
    for lane, m_ref in enumerate(m_refs):
        flat = m_ref.reshape(rows * slabs, LANES)
        cols = slice(lane * LANES, (lane + 1) * LANES)
        for slot, side in enumerate(sides):
            first = 0 if slabs == count else (half_ref[0] ^ side) * count
            for s in range(count):
                o_ref[s, slot, :, cols] = flat[pl.ds(first + s, rows, stride=slabs), :]


def relay(half, measured, sides, first_view, views, count, into=None, slot=0, slots=None, after=None, cost=SMALL):
    segs, _, inner, slabs, bins = measured.shape
    rows = segs * inner
    slots = len(sides) if slots is None else slots
    specs = [
        pl.BlockSpec((segs, 1, inner, slabs, LANES), lambda v, lane=lane: (0, first_view + v, 0, 0, lane))
        for lane in range(lane_blocks(bins))
    ]
    lanes = len(specs)
    operands = [half] + [measured] * lanes
    aliases = {}
    if into is not None:
        aliases = {len(operands): 0}
        operands.append(into)
    if after is not None:
        operands.append(after)
    specs = [SMEM] + specs + [pl.BlockSpec(memory_space=pl.ANY)] * (len(operands) - 1 - lanes)
    return pl.pallas_call(
        functools.partial(relay_kernel, sides, lanes),
        grid=(views,),
        in_specs=specs,
        out_specs=pl.BlockSpec((count, len(sides), rows, bins), lambda v: (0, v * slots // len(sides) + slot, 0, 0)),
        out_shape=jax.ShapeDtypeStruct((count, views * slots, rows, bins), f32),
        input_output_aliases=aliases,
        compiler_params=params(52),
        cost_estimate=cost,
    )(*operands)


def split_two(x):
    hi = x.astype(bf16)
    return hi, (x - hi.astype(f32)).astype(bf16)


def axial_entries(weight, slices, margin, segs, inner, row, column):
    place = jnp.where(
        column < slices, column + margin, jnp.where(column < slices + margin, column - slices, column)
    )
    group = (row // inner) % segs
    tap = place - (row // (inner * segs) * inner + row % inner)
    entries = jnp.zeros(row.shape, f32)
    for k in range(2 * margin + 1):
        value = jnp.full(row.shape, weight(0, k), f32)
        for g in range(1, segs):
            value = jnp.where(group == g, weight(g, k), value)
        entries = jnp.where(tap == k, value, entries)
    return entries


def setup_kernel(slices, segs, inner, halves, me_ref, k_ref, t_ref, c_ref, o_ref, op_ref, opt_ref):
    lanes, depth = t_ref.shape
    views = o_ref.shape[0]
    bins = c_ref.shape[-1]
    taps = k_ref.shape[1]
    margin = (taps - 1) // 2
    first_row = me_ref[0] % halves * segs
    turned = me_ref[0] >= halves

    def weight(g, k):
        return jnp.where(turned, k_ref[first_row + g, taps - 1 - k], k_ref[first_row + g, k])

    def ids(shape, dim):
        return lax.broadcasted_iota(jnp.int32, shape, dim)

    shape = op_ref.shape
    op_ref[...] = axial_entries(weight, slices, margin, segs, inner, ids(shape, 0), ids(shape, 1))
    _, ext, part = opt_ref.shape
    for h in range(2):
        opt_ref[h] = axial_entries(
            weight, slices, margin, segs, inner, ids((ext, part), 1) + h * part, ids((ext, part), 0)
        )

    table = t_ref[...].astype(f32)
    first = table.astype(bf16)
    rest = table - first.astype(f32)
    second = rest.astype(bf16)
    third = (rest - second.astype(f32)).astype(bf16)
    pieces = jnp.concatenate([first, second, third], axis=0)
    depth_ids = ids((depth, bins), 0)
    lane_ids = ids((lanes, bins), 0)

    def look(index):
        row = index // lanes
        hot = jnp.where(depth_ids == row, 1.0, 0.0).astype(bf16)
        got = jnp.dot(pieces, hot, preferred_element_type=f32)
        value = got[:lanes] + got[lanes : 2 * lanes] + got[2 * lanes :]
        return jnp.sum(jnp.where(lane_ids == index - row * lanes, value, 0.0), axis=0, keepdims=True)

    def one_view(v, carry):
        first_factor = 1.0 + dead_time_tau * look(c_ref[0, v])
        second_factor = 1.0 + dead_time_tau * look(c_ref[1, v])
        o_ref[v] = 1.0 / (first_factor * second_factor)
        return carry

    lax.fori_loop(0, views, one_view, 0)


def setup(me, kernel, dead_counts, crystals, slices, segs, inner, halves):
    _, views, bins = crystals.shape
    taps = kernel.shape[1]
    rows = slices * segs
    ext = slices + taps - 1 + 8
    table = dead_counts.reshape(-1, LANES).T
    return pl.pallas_call(
        functools.partial(setup_kernel, slices, segs, inner, halves),
        in_specs=[SMEM, SMEM, VMEM, VMEM],
        out_specs=[VMEM] * 3,
        out_shape=[
            jax.ShapeDtypeStruct((views, 1, bins), f32),
            jax.ShapeDtypeStruct((rows, ext), f32),
            jax.ShapeDtypeStruct((2, ext, rows // 2), f32),
        ],
        compiler_params=params(24),
        cost_estimate=SMALL,
    )(me, kernel, table, crystals.reshape(2, views, 1, bins))


def forward_kernel(op_ref, ext_ref, foot_hbm, eff_ref, _, *refs):
    lanes = (len(refs) - 4) // 2
    rand_refs, o_ref, foot_ref, rows_ref = refs[:lanes], refs[lanes], refs[lanes + 1], refs[lanes + 2]
    order_refs, sems = refs[lanes + 3 : -1], refs[-1]
    segs, _, slices, _ = rand_refs[0].shape
    pixels = ext_ref.shape[1]
    inner = 2
    count = slices // inner
    view = pl.program_id(0)

    def fetch(v):
        return pltpu.make_async_copy(foot_hbm.at[v], foot_ref.at[v], sems.at[v])

    @pl.when(view == 0)
    def _():
        for v in range(foot_ref.shape[0]):
            fetch(v).start()
        rows_ref[...] = jnp.dot(
            op_ref[...], ext_ref[...], preferred_element_type=f32, precision=lax.Precision.HIGHEST
        ).astype(bf16)

    fetch(view).wait()
    projected = jnp.dot(rows_ref[...], foot_ref[view], preferred_element_type=f32) * (1.0 / pixels)
    for lane in range(lanes):
        flat = rand_refs[lane].reshape(segs * slices, LANES)
        order_ref = order_refs[lane]
        for g in range(segs):
            for a in range(inner):
                got = flat[pl.ds(g * slices + a, count, stride=inner), :].astype(f32)
                order_ref[pl.ds(g * inner + a, count, stride=segs * inner), :] = 0.25 * (got + 1.0)
        cols = slice(lane * LANES, (lane + 1) * LANES)
        eff = eff_ref[0, :, cols]
        value = eff / (eff * projected[:, cols] + order_ref[...])
        o_ref[0, :, :, :, cols] = value.reshape(*o_ref.shape[1:4], LANES)


def forward(operator, extended, footprint, randoms, efficiency, after):
    segs, views, slices, bins = randoms.shape
    pixels = footprint.shape[1]
    rows = segs * slices
    inner = 2 * segs
    lanes = [
        pl.BlockSpec((segs, 1, slices, LANES), lambda v, lane=lane: (0, v, 0, lane))
        for lane in range(lane_blocks(bins))
    ]
    return pl.pallas_call(
        forward_kernel,
        grid=(views,),
        in_specs=[
            VMEM,
            VMEM,
            pl.BlockSpec(memory_space=pltpu.HBM),
            pl.BlockSpec((1, 1, bins), lambda v: (v, 0, 0)),
            pl.BlockSpec(memory_space=pl.ANY),
        ]
        + lanes,
        out_specs=pl.BlockSpec((1, 2, rows // inner // 2, inner, bins), lambda v: (v, 0, 0, 0, 0)),
        out_shape=jax.ShapeDtypeStruct((views, 2, rows // inner // 2, inner, bins), f32),
        scratch_shapes=[pltpu.VMEM(footprint.shape, footprint.dtype), pltpu.VMEM((rows, pixels), bf16)]
        + [pltpu.VMEM((rows, LANES), f32)] * len(lanes)
        + [pltpu.SemaphoreType.DMA((views,))],
        compiler_params=params(40),
        cost_estimate=SMALL,
    )(operator, extended, footprint, efficiency, after, *[randoms] * len(lanes))


def back_project(operator, weighted, foot):
    ext = operator.shape[0]
    hi, lo = split_two(operator)
    both = jnp.dot(jnp.concatenate([hi, lo], axis=0), weighted, preferred_element_type=f32)
    hi, lo = split_two(both[:ext] + both[ext:])
    spread = lax.dot_general(
        jnp.concatenate([hi, lo], axis=0), foot, (((1,), (1,)), ((), ())), preferred_element_type=f32
    )
    return spread[:ext] + spread[ext:]


def ratio(factor, rows_in):
    scaled = factor * rows_in
    return scaled.reshape(-1, scaled.shape[-1]).astype(bf16)


def start_all(copies):
    for copy in copies:
        copy.start()


def back_staged_kernel(
    edge, half_ref, op_ref, staged_hbm, part_ref, factor_hbm, foot_hbm, acc_ref, own_ref, factor_ref, foot_ref, sems
):
    half = half_ref[0]
    views, count, inner, bins = own_ref.shape
    firsts = factor_hbm.shape[0] - views

    def copies(v):
        return [
            pltpu.make_async_copy(staged_hbm.at[:, 2 * v], own_ref.at[v], sems.at[v, 0]),
            pltpu.make_async_copy(factor_hbm.at[firsts + v], factor_ref.at[v], sems.at[v, 1]),
            pltpu.make_async_copy(foot_hbm.at[firsts + v], foot_ref.at[v], sems.at[v, 2]),
        ]

    for v in range(views):
        start_all(copies(v))
    middles = (part_ref.shape[0] - 2 * edge * views) // (count - 2 * edge)
    operator = jnp.concatenate([op_ref[half], op_ref[1 - half]], axis=1)
    for v in range(views):
        for copy in copies(v):
            copy.wait()
        far = factor_ref[v, 1 - half]
        own = ratio(factor_ref[v, half], own_ref[v])
        low = ratio(far[:edge], part_ref[2 * edge * v : 2 * edge * v + edge])
        high = ratio(far[count - edge :], part_ref[2 * edge * v + edge : 2 * edge * (v + 1)])
        if v < middles:
            first = 2 * edge * views + (count - 2 * edge) * v
            middle = ratio(far[edge : count - edge], part_ref[first : first + count - 2 * edge])
        else:
            middle = jnp.zeros(((count - 2 * edge) * inner, bins), bf16)
        spread = back_project(operator, jnp.concatenate([own, low, middle, high], axis=0), foot_ref[v])
        if v == 0:
            acc_ref[...] = spread
        else:
            acc_ref[...] += spread


def back_staged(half, operator, staged, part, factor, footprint, edge):
    ext = operator.shape[1]
    count, slots, inner, bins = staged.shape
    views = slots // 2
    pixels = footprint.shape[1]
    return pl.pallas_call(
        functools.partial(back_staged_kernel, edge),
        in_specs=[SMEM, VMEM, HBM, VMEM, HBM, HBM],
        out_specs=VMEM,
        out_shape=jax.ShapeDtypeStruct((ext, pixels), f32),
        scratch_shapes=[
            pltpu.VMEM((views, count, inner, bins), f32),
            pltpu.VMEM((views, 2, count, inner, bins), f32),
            pltpu.VMEM((views, pixels, bins), bf16),
            pltpu.SemaphoreType.DMA((views, 3)),
        ],
        compiler_params=params(52),
        cost_estimate=LARGE,
    )(half, operator, staged, part, factor, footprint)


def back_near_kernel(
    half_ref, me_ref, op_ref, near_hbm, factor_hbm, foot_hbm, in_ref, acc_ref, keep_ref, give_ref, *scratch
):
    near_ref, factor_ref, foot_ref, sum_ref, sems = scratch
    half = half_ref[0]
    views = near_ref.shape[0]

    def copies(v):
        return [
            pltpu.make_async_copy(near_hbm.at[:, pl.ds(2 * v, 2)], near_ref.at[v], sems.at[v, 0]),
            pltpu.make_async_copy(factor_hbm.at[v], factor_ref.at[v], sems.at[v, 1]),
            pltpu.make_async_copy(foot_hbm.at[v], foot_ref.at[v], sems.at[v, 2]),
        ]

    for v in range(views):
        start_all(copies(v))
    operator = jnp.concatenate([op_ref[half], op_ref[1 - half]], axis=1)
    sum_ref[...] = in_ref[...]
    for v in range(views):
        for copy in copies(v):
            copy.wait()
        own = ratio(factor_ref[v, half], near_ref[v, :, 0])
        far = ratio(factor_ref[v, 1 - half], near_ref[v, :, 1])
        sum_ref[...] += back_project(operator, jnp.concatenate([own, far], axis=0), foot_ref[v])
    slices, pixels = acc_ref.shape
    margin, width = keep_ref.shape[2:]
    acc_ref[...] = sum_ref[:slices]
    core = me_ref[0] % 2
    for k in range(4):
        for c in range(2):
            block = me_ref[0] ^ (2 * k + c)
            cols = pl.ds(pl.multiple_of(block * width, width), width)
            pair = sum_ref[slices : slices + 2 * margin, cols] * (1.0 / pixels)
            up, down = pair[:margin], pair[margin:]
            keep_ref[c, k] = jnp.where(core == 0, down, up)
            give_ref[c, k] = jnp.where(core == 0, up, down)


def back_near(half, me, operator, near, factor, footprint, acc, slices, margin):
    count, slots, inner, bins = near.shape
    views = slots // 2
    pixels = footprint.shape[1]
    halo = jax.ShapeDtypeStruct((2, 4, margin, pixels // 8), f32)
    return pl.pallas_call(
        back_near_kernel,
        in_specs=[SMEM, SMEM, VMEM, HBM, HBM, HBM, VMEM],
        out_specs=[VMEM] * 3,
        out_shape=[jax.ShapeDtypeStruct((slices, pixels), f32), halo, halo],
        scratch_shapes=[
            pltpu.VMEM((views, count, 2, inner, bins), f32),
            pltpu.VMEM((views, 2, count, inner, bins), f32),
            pltpu.VMEM((views, pixels, bins), bf16),
            pltpu.VMEM(acc.shape, f32),
            pltpu.SemaphoreType.DMA((views, 3)),
        ],
        compiler_params=params(52),
        cost_estimate=SMALL,
    )(half, me, operator, near, factor, footprint, acc)


def pieces_kernel(edge, views, staged_hbm, part_ref, last_ref, sems):
    count = staged_hbm.shape[0]
    middle = count - 2 * edge
    copies = []

    def add(slices, v, target):
        copies.append(pltpu.make_async_copy(staged_hbm.at[slices, 2 * v + 1], target, sems.at[len(copies)]))

    lasts = last_ref.shape[1]
    for v in range(views):
        add(pl.ds(0, edge), v, part_ref.at[pl.ds(2 * edge * v, edge)])
        add(pl.ds(count - edge, edge), v, part_ref.at[pl.ds(2 * edge * v + edge, edge)])
        if v < views - lasts:
            add(pl.ds(edge, middle), v, part_ref.at[pl.ds(2 * edge * views + middle * v, middle)])
        else:
            add(pl.ds(edge, middle), v, last_ref.at[:, v - views + lasts])
    start_all(copies)
    for copy in copies:
        copy.wait()


def pieces(staged, edge, lasts):
    count, slots, inner, bins = staged.shape
    views = slots // 2
    middle = count - 2 * edge
    part = 2 * edge * views + middle * (views - lasts)
    return pl.pallas_call(
        functools.partial(pieces_kernel, edge, views),
        in_specs=[HBM],
        out_specs=[VMEM] * 2,
        out_shape=[
            pltpu.VMEM((part, inner, bins), f32),
            pltpu.VMEM((middle, lasts, inner, bins), f32),
        ],
        scratch_shapes=[pltpu.SemaphoreType.DMA((3 * views,))],
        compiler_params=params(16),
        cost_estimate=SMALL,
    )(staged)


def mark_kernel(x_ref, o_ref):
    o_ref[...] = jnp.zeros_like(o_ref)


def mark(x):
    return pl.pallas_call(
        mark_kernel,
        in_specs=[pl.BlockSpec(memory_space=pl.ANY)],
        out_specs=VMEM,
        out_shape=jax.ShapeDtypeStruct((8, LANES), f32),
        compiler_params=params(16),
        cost_estimate=LARGE,
    )(x)


def back_last_kernel(half_ref, me_ref, op_ref, x_ref, factor_ref, foot_ref, in_ref, *refs):
    mine_refs, other_ref, acc_ref = refs[:4], refs[4], refs[5]
    slices, pixels = acc_ref.shape
    middle, views, inner, bins = x_ref.shape
    count = factor_ref.shape[2]
    edge = (count - middle) // 2
    far = 1 - half_ref[0]
    gap = jnp.zeros((edge * inner, bins), bf16)
    operator = op_ref[far, :slices]
    acc_ref[...] = in_ref[...]
    for v in range(views):
        weighted = ratio(factor_ref[v, far, edge : count - edge], x_ref[:, v])
        acc_ref[...] += back_project(operator, jnp.concatenate([gap, weighted, gap], axis=0), foot_ref[v])
    width = mine_refs[0].shape[1]
    for k in range(4):
        for c in range(2):
            block = me_ref[0] ^ (2 * k + c)
            part = acc_ref[:, pl.ds(pl.multiple_of(block * width, width), width)] * (1.0 / pixels)
            if c == 0:
                mine_refs[k][...] = part
            else:
                other_ref[k] = part


def back_last(half, me, operator, rows_in, factor, footprint, acc):
    slices, pixels = acc.shape
    width = pixels // 8
    return pl.pallas_call(
        back_last_kernel,
        in_specs=[SMEM, SMEM] + [VMEM] * 5,
        out_specs=[VMEM] * 5,
        out_shape=[pltpu.VMEM((slices, width), f32)] * 4 + [pltpu.VMEM((4, slices, width), f32)],
        scratch_shapes=[pltpu.VMEM((slices, pixels), f32)],
        compiler_params=params(24),
        cost_estimate=SMALL,
    )(half, me, operator, rows_in, factor, footprint, acc)


def pair_kernel(me_ref, *refs):
    mine_refs, theirs_ref, halo_ref, across_ref, out_refs = refs[:4], refs[4], refs[5], refs[6], refs[7:]
    core = me_ref[0] % 2
    slices, _ = mine_refs[0].shape
    margin = halo_ref.shape[2]
    for k in range(4):
        here, there = halo_ref[0, k], across_ref[k]
        above = jnp.where(core == 0, here, there)
        below = jnp.where(core == 0, there, here)
        out_refs[k][...] = mine_refs[k][...] + theirs_ref[k]
        out_refs[k][:margin] += above
        out_refs[k][slices - margin :] += below


def pair_sum(me, mine, theirs, halo, across):
    return pl.pallas_call(
        pair_kernel,
        in_specs=[SMEM] + [VMEM] * 7,
        out_specs=[VMEM] * 4,
        out_shape=[pltpu.VMEM(x.shape, f32) for x in mine],
        compiler_params=params(16),
        cost_estimate=SMALL,
    )(me, *mine, theirs, halo, across)


def assemble_kernel(me_ref, *refs):
    near_refs, far_ref, o_ref = refs[:4], refs[4], refs[5]
    width = near_refs[0].shape[1]
    for k in range(4):
        for c in range(2):
            block = me_ref[0] ^ (2 * k + c)
            part = near_refs[k][...] if c == 0 else far_ref[k]
            o_ref[:, pl.ds(pl.multiple_of(block * width, width), width)] = part


def assemble(me, near, far):
    slices, width = near[0].shape
    return pl.pallas_call(
        assemble_kernel,
        in_specs=[SMEM] + [VMEM] * 5,
        out_specs=VMEM,
        out_shape=jax.ShapeDtypeStruct((slices, width * 8), f32),
        compiler_params=params(16),
    )(me, *near, far)


def local(activity, measured, randoms, footprint, kernel, dead_counts, crystals, sensitivity):
    segs, views, inner, slabs, bins = measured.shape
    slices, pixels = activity.shape
    taps = kernel.shape[1]
    margin = (taps - 1) // 2
    width = pixels // 8
    group = lax.axis_index("seg")
    me = group.astype(jnp.int32).reshape(1)
    halves = lax.axis_size("seg") // 2

    def swap(x, k):
        return lax.ppermute(x, "seg", [(i, i ^ k) for i in range(2 * halves)])

    def outward(x):
        pairs = []
        for j in range(2 * halves):
            for i in range(slabs - 1):
                source, target = (i, i + 1) if j % 2 == 0 else (i + 1, i)
                pairs.append((j * slabs + source, j * slabs + target))
        return lax.ppermute(x, ("seg", "slab"), pairs)

    count = slabs // 2
    half = (lax.axis_index("slab").astype(jnp.int32) // count).reshape(1)
    edge = margin // inner
    firsts = views // 2
    lasts = 2

    def cross(x):
        return lax.ppermute(x, "slab", [(i, (i + count) % slabs) for i in range(slabs)])

    def exchange(x):
        groups = [[h * count + i for i in range(count)] for h in range(2)]
        return lax.all_to_all(x, "slab", split_axis=0, concat_axis=0, tiled=True, axis_index_groups=groups)

    ext = slices + 2 * margin
    early = lax.dynamic_slice_in_dim(measured[:, :firsts], (1 - half[0]) * count, count, 3)
    early = cross(early)
    staged = relay(half, measured, (0, 1), firsts, views - firsts, count)
    staged, near_activity = lax.optimization_barrier((staged, activity))
    staged = exchange(staged)
    near = relay(half, measured, (0,), 0, firsts, count, slots=2, cost=SMALL)
    efficiency, operator, operator_t = setup(me, kernel, dead_counts, crystals, slices, segs, inner, halves)
    even = group % 2 == 0
    halo = outward(jnp.where(even, near_activity[slices - margin :], near_activity[:margin]))
    across = swap(halo, 1)
    extended = jnp.concatenate(
        [
            activity,
            jnp.where(even, halo, across),
            jnp.where(even, across, halo),
            jnp.zeros((8, pixels), f32),
        ],
        axis=0,
    )

    staged, near, begun = lax.optimization_barrier((staged, near, mark(early)))
    part, rows_last = pieces(staged, edge, lasts)
    part = cross(part)
    near = relay(half, early, (1,), 0, firsts, count, into=near, slot=1, slots=2, after=begun)
    rows_last, near = lax.optimization_barrier((rows_last, near))
    rows_last = cross(rows_last)
    near = exchange(near)
    factor = forward(operator, extended, footprint, randoms, efficiency, begun)

    last_factor, last_foot = factor[views - lasts :], footprint[views - lasts :]
    acc = back_staged(half, operator_t, staged, part, factor, footprint, edge)
    acc, last_factor, last_foot = lax.optimization_barrier((acc, last_factor, last_foot))
    acc, keep, give = back_near(half, me, operator_t, near, factor, footprint, acc, slices, margin)
    halo = outward(keep + swap(give, 1)[::-1])
    across = swap(halo[1], 1)
    *mine, other = back_last(half, me, operator_t, rows_last, last_factor, last_foot, acc)
    pair = pair_sum(me, mine, swap(other, 1), halo, across)
    total = pair[0]
    for k in range(1, 4):
        total = total + swap(pair[k], 2 * k)
    start = group * width
    gain = lax.dynamic_slice_in_dim(activity, start, width, 1) / lax.dynamic_slice_in_dim(
        sensitivity, start, width, 1
    )
    block = total * gain
    near = [block] + [swap(block, 2 * k) for k in range(1, 4)]
    far = swap(jnp.stack(near), 1)
    return assemble(me, near, far)


def solution(mesh):
    placed = (
        P("slab", None),
        P("seg", None, "slab", None, None),
        P("seg", None, "slab", None),
        P(),
        P(),
        P(),
        P(),
        P("slab", None),
    )
    return jax.shard_map(
        local, mesh=mesh, in_specs=placed, out_specs=P("slab", None), check_vma=False
    )
```

```python
import functools
import jax
import jax.numpy as jnp
from jax import lax
from jax.experimental import pallas as pl
from jax.experimental.pallas import tpu as pltpu
from jax.sharding import PartitionSpec as P

dead_time_tau = 0.001
f32 = jnp.float32
bf16 = jnp.bfloat16
LANES = 128
MIRROR = 6
VMEM = pl.BlockSpec(memory_space=pltpu.VMEM)
SMEM = pl.BlockSpec(memory_space=pltpu.SMEM)
HBM = pl.BlockSpec(memory_space=pltpu.HBM)
SMALL = pl.CostEstimate(flops=1, bytes_accessed=1, transcendentals=0)
LARGE = pl.CostEstimate(flops=10**12, bytes_accessed=1 << 20, transcendentals=0)


def params(mib):
    return pltpu.CompilerParams(vmem_limit_bytes=mib << 20)


def lane_blocks(bins):
    return bins // LANES


def relay_kernel(sides, lanes, half_ref, *refs):
    m_refs, o_ref = refs[:lanes], refs[-1]
    segs, _, inner, slabs, _ = m_refs[0].shape
    rows = segs * inner
    count = o_ref.shape[0]
    for lane, m_ref in enumerate(m_refs):
        flat = m_ref.reshape(rows * slabs, LANES)
        cols = slice(lane * LANES, (lane + 1) * LANES)
        for slot, side in enumerate(sides):
            first = 0 if slabs == count else (half_ref[0] ^ side) * count
            for s in range(count):
                o_ref[s, slot, :, cols] = flat[pl.ds(first + s, rows, stride=slabs), :]


def relay(half, measured, sides, first_view, views, count, into=None, slot=0, slots=None, after=(), cost=SMALL):
    segs, _, inner, slabs, bins = measured.shape
    rows = segs * inner
    slots = len(sides) if slots is None else slots
    specs = [
        pl.BlockSpec((segs, 1, inner, slabs, LANES), lambda v, lane=lane: (0, first_view + v, 0, 0, lane))
        for lane in range(lane_blocks(bins))
    ]
    lanes = len(specs)
    operands = [half] + [measured] * lanes
    aliases = {}
    if into is not None:
        aliases = {len(operands): 0}
        operands.append(into)
    operands += after
    specs = [SMEM] + specs + [pl.BlockSpec(memory_space=pl.ANY)] * (len(operands) - 1 - lanes)
    return pl.pallas_call(
        functools.partial(relay_kernel, sides, lanes),
        grid=(views,),
        in_specs=specs,
        out_specs=pl.BlockSpec((count, len(sides), rows, bins), lambda v: (0, v * slots // len(sides) + slot, 0, 0)),
        out_shape=jax.ShapeDtypeStruct((count, views * slots, rows, bins), f32),
        input_output_aliases=aliases,
        compiler_params=params(52),
        cost_estimate=cost,
    )(*operands)


def split_two(x):
    hi = x.astype(bf16)
    return hi, (x - hi.astype(f32)).astype(bf16)


def axial_entries(weight, slices, margin, segs, inner, row, column):
    place = jnp.where(
        column < slices, column + margin, jnp.where(column < slices + margin, column - slices, column)
    )
    group = (row // inner) % segs
    tap = place - (row // (inner * segs) * inner + row % inner)
    entries = jnp.zeros(row.shape, f32)
    for k in range(2 * margin + 1):
        value = jnp.full(row.shape, weight(0, k), f32)
        for g in range(1, segs):
            value = jnp.where(group == g, weight(g, k), value)
        entries = jnp.where(tap == k, value, entries)
    return entries


def setup_kernel(slices, segs, inner, halves, me_ref, k_ref, t_ref, c_ref, o_ref, op_ref, opt_ref):
    lanes, depth = t_ref.shape
    views = o_ref.shape[0]
    bins = c_ref.shape[-1]
    taps = k_ref.shape[1]
    margin = (taps - 1) // 2
    first_row = me_ref[0] % halves * segs
    turned = me_ref[0] >= halves

    def weight(g, k):
        return jnp.where(turned, k_ref[first_row + g, taps - 1 - k], k_ref[first_row + g, k])

    def ids(shape, dim):
        return lax.broadcasted_iota(jnp.int32, shape, dim)

    shape = op_ref.shape
    op_ref[...] = axial_entries(weight, slices, margin, segs, inner, ids(shape, 0), ids(shape, 1))
    _, ext, part = opt_ref.shape
    for h in range(2):
        opt_ref[h] = axial_entries(
            weight, slices, margin, segs, inner, ids((ext, part), 1) + h * part, ids((ext, part), 0)
        )

    table = t_ref[...].astype(f32)
    first = table.astype(bf16)
    rest = table - first.astype(f32)
    second = rest.astype(bf16)
    third = (rest - second.astype(f32)).astype(bf16)
    pieces = jnp.concatenate([first, second, third], axis=0)
    depth_ids = ids((depth, bins), 0)
    lane_ids = ids((lanes, bins), 0)

    def look(index):
        row = index // lanes
        hot = jnp.where(depth_ids == row, 1.0, 0.0).astype(bf16)
        got = jnp.dot(pieces, hot, preferred_element_type=f32)
        value = got[:lanes] + got[lanes : 2 * lanes] + got[2 * lanes :]
        return jnp.sum(jnp.where(lane_ids == index - row * lanes, value, 0.0), axis=0, keepdims=True)

    def one_view(v, carry):
        first_factor = 1.0 + dead_time_tau * look(c_ref[0, v])
        second_factor = 1.0 + dead_time_tau * look(c_ref[1, v])
        o_ref[v] = 1.0 / (first_factor * second_factor)
        return carry

    lax.fori_loop(0, views, one_view, 0)


def setup(me, kernel, dead_counts, crystals, slices, segs, inner, halves):
    _, views, bins = crystals.shape
    taps = kernel.shape[1]
    rows = slices * segs
    ext = slices + taps - 1 + 8
    table = dead_counts.reshape(-1, LANES).T
    return pl.pallas_call(
        functools.partial(setup_kernel, slices, segs, inner, halves),
        in_specs=[SMEM, SMEM, VMEM, VMEM],
        out_specs=[VMEM] * 3,
        out_shape=[
            jax.ShapeDtypeStruct((views, 1, bins), f32),
            jax.ShapeDtypeStruct((rows, ext), f32),
            jax.ShapeDtypeStruct((2, ext, rows // 2), f32),
        ],
        compiler_params=params(24),
        cost_estimate=SMALL,
    )(me, kernel, table, crystals.reshape(2, views, 1, bins))


def forward_kernel(op_ref, act_ref, above_ref, below_ref, foot_hbm, eff_ref, *refs):
    lanes = (len(refs) - 5) // 2
    rand_refs, o_ref, foot_ref, rows_ref = refs[:lanes], refs[lanes], refs[lanes + 1], refs[lanes + 2]
    order_refs, ext_ref, sems = refs[lanes + 3 : -2], refs[-2], refs[-1]
    segs, _, slices, _ = rand_refs[0].shape
    pixels = ext_ref.shape[1]
    margin = above_ref.shape[0]
    inner = 2
    count = slices // inner
    view = pl.program_id(0)

    def fetch(v):
        return pltpu.make_async_copy(foot_hbm.at[v], foot_ref.at[v], sems.at[v])

    @pl.when(view == 0)
    def _():
        for v in range(foot_ref.shape[0]):
            fetch(v).start()
        ext_ref[...] = jnp.zeros_like(ext_ref)
        ext_ref[:slices] = act_ref[...]
        ext_ref[slices : slices + margin] = above_ref[...]
        ext_ref[slices + margin : slices + 2 * margin] = below_ref[...]
        rows_ref[...] = jnp.dot(
            op_ref[...], ext_ref[...], preferred_element_type=f32, precision=lax.Precision.HIGHEST
        ).astype(bf16)

    fetch(view).wait()
    projected = jnp.dot(rows_ref[...], foot_ref[view], preferred_element_type=f32) * (1.0 / pixels)
    for lane in range(lanes):
        flat = rand_refs[lane].reshape(segs * slices, LANES)
        order_ref = order_refs[lane]
        for g in range(segs):
            for a in range(inner):
                got = flat[pl.ds(g * slices + a, count, stride=inner), :].astype(f32)
                order_ref[pl.ds(g * inner + a, count, stride=segs * inner), :] = 0.25 * (got + 1.0)
        cols = slice(lane * LANES, (lane + 1) * LANES)
        eff = eff_ref[0, :, cols]
        value = eff / (eff * projected[:, cols] + order_ref[...])
        o_ref[0, :, :, :, cols] = value.reshape(*o_ref.shape[1:4], LANES)


def forward(operator, activity, above, below, footprint, randoms, efficiency):
    segs, views, slices, bins = randoms.shape
    pixels = footprint.shape[1]
    rows = segs * slices
    inner = 2 * segs
    lanes = [
        pl.BlockSpec((segs, 1, slices, LANES), lambda v, lane=lane: (0, v, 0, lane))
        for lane in range(lane_blocks(bins))
    ]
    return pl.pallas_call(
        forward_kernel,
        grid=(views,),
        in_specs=[
            VMEM,
            VMEM,
            VMEM,
            VMEM,
            HBM,
            pl.BlockSpec((1, 1, bins), lambda v: (v, 0, 0)),
        ]
        + lanes,
        out_specs=pl.BlockSpec((1, 2, rows // inner // 2, inner, bins), lambda v: (v, 0, 0, 0, 0)),
        out_shape=jax.ShapeDtypeStruct((views, 2, rows // inner // 2, inner, bins), f32),
        scratch_shapes=[pltpu.VMEM(footprint.shape, footprint.dtype), pltpu.VMEM((rows, pixels), bf16)]
        + [pltpu.VMEM((rows, LANES), f32)] * len(lanes)
        + [pltpu.VMEM((operator.shape[1], pixels), f32), pltpu.SemaphoreType.DMA((views,))],
        compiler_params=params(40),
        cost_estimate=SMALL,
    )(operator, activity, above, below, footprint, efficiency, *[randoms] * len(lanes))


def back_project(operator, weighted, foot):
    ext = operator.shape[0]
    hi, lo = split_two(operator)
    both = jnp.dot(jnp.concatenate([hi, lo], axis=0), weighted, preferred_element_type=f32)
    hi, lo = split_two(both[:ext] + both[ext:])
    spread = lax.dot_general(
        jnp.concatenate([hi, lo], axis=0), foot, (((1,), (1,)), ((), ())), preferred_element_type=f32
    )
    return spread[:ext] + spread[ext:]


def ratio(factor, rows_in):
    scaled = factor * rows_in
    return scaled.reshape(-1, scaled.shape[-1]).astype(bf16)


def start_all(copies):
    for copy in copies:
        copy.start()


def back_staged_kernel(
    edge,
    half_ref,
    op_ref,
    staged_hbm,
    part_ref,
    factor_hbm,
    foot_hbm,
    acc_ref,
    last_factor_ref,
    last_foot_ref,
    own_ref,
    factor_ref,
    foot_ref,
    sems,
):
    half = half_ref[0]
    views, count, inner, bins = own_ref.shape
    firsts = factor_hbm.shape[0] - views
    middles = foot_ref.shape[0]

    def place(v):
        if v < middles:
            return factor_ref.at[v], foot_ref.at[v]
        return last_factor_ref.at[v - middles], last_foot_ref.at[v - middles]

    def copies(v):
        factor, foot = place(v)
        return [
            pltpu.make_async_copy(staged_hbm.at[:, 2 * v], own_ref.at[v], sems.at[v, 0]),
            pltpu.make_async_copy(factor_hbm.at[firsts + v], factor, sems.at[v, 1]),
            pltpu.make_async_copy(foot_hbm.at[firsts + v], foot, sems.at[v, 2]),
        ]

    for v in range(views):
        start_all(copies(v))
    operator = jnp.concatenate([op_ref[half], op_ref[1 - half]], axis=1)
    for v in range(views):
        for copy in copies(v):
            copy.wait()
        factor, foot = place(v)
        far = factor[1 - half]
        own = ratio(factor[half], own_ref[v])
        low = ratio(far[:edge], part_ref[2 * edge * v : 2 * edge * v + edge])
        high = ratio(far[count - edge :], part_ref[2 * edge * v + edge : 2 * edge * (v + 1)])
        if v < middles:
            first = 2 * edge * views + (count - 2 * edge) * v
            middle = ratio(far[edge : count - edge], part_ref[first : first + count - 2 * edge])
        else:
            middle = jnp.zeros(((count - 2 * edge) * inner, bins), bf16)
        spread = back_project(operator, jnp.concatenate([own, low, middle, high], axis=0), foot[...])
        if v == 0:
            acc_ref[...] = spread
        else:
            acc_ref[...] += spread


def back_staged(half, operator, staged, part, factor, footprint, edge, lasts):
    ext = operator.shape[1]
    count, slots, inner, bins = staged.shape
    views = slots // 2
    pixels = footprint.shape[1]
    return pl.pallas_call(
        functools.partial(back_staged_kernel, edge),
        in_specs=[SMEM, VMEM, HBM, VMEM, HBM, HBM],
        out_specs=[VMEM] * 3,
        out_shape=[
            jax.ShapeDtypeStruct((ext, pixels), f32),
            pltpu.VMEM((lasts, 2, count, inner, bins), f32),
            pltpu.VMEM((lasts, pixels, bins), bf16),
        ],
        scratch_shapes=[
            pltpu.VMEM((views, count, inner, bins), f32),
            pltpu.VMEM((views - lasts, 2, count, inner, bins), f32),
            pltpu.VMEM((views - lasts, pixels, bins), bf16),
            pltpu.SemaphoreType.DMA((views, 3)),
        ],
        compiler_params=params(52),
        cost_estimate=LARGE,
    )(half, operator, staged, part, factor, footprint)


def back_near_kernel(
    half_ref, me_ref, op_ref, near_hbm, factor_hbm, foot_hbm, in_ref, acc_ref, keep_ref, give_ref, *scratch
):
    near_ref, factor_ref, foot_ref, sum_ref, sems = scratch
    half = half_ref[0]
    views = near_ref.shape[0]

    def copies(v):
        return [
            pltpu.make_async_copy(near_hbm.at[:, pl.ds(2 * v, 2)], near_ref.at[v], sems.at[v, 0]),
            pltpu.make_async_copy(factor_hbm.at[v], factor_ref.at[v], sems.at[v, 1]),
            pltpu.make_async_copy(foot_hbm.at[v], foot_ref.at[v], sems.at[v, 2]),
        ]

    for v in range(views):
        start_all(copies(v))
    operator = jnp.concatenate([op_ref[half], op_ref[1 - half]], axis=1)
    sum_ref[...] = in_ref[...]
    for v in range(views):
        for copy in copies(v):
            copy.wait()
        own = ratio(factor_ref[v, half], near_ref[v, :, 0])
        far = ratio(factor_ref[v, 1 - half], near_ref[v, :, 1])
        sum_ref[...] += back_project(operator, jnp.concatenate([own, far], axis=0), foot_ref[v])
    slices, pixels = acc_ref.shape
    margin, width = keep_ref.shape[2:]
    acc_ref[...] = sum_ref[:slices]
    core = me_ref[0] % 2
    for k in range(4):
        for c in range(2):
            block = me_ref[0] ^ (2 * k + c)
            cols = pl.ds(pl.multiple_of(block * width, width), width)
            pair = sum_ref[slices : slices + 2 * margin, cols] * (1.0 / pixels)
            up, down = pair[:margin], pair[margin:]
            keep_ref[c, k] = jnp.where(core == 0, down, up)
            give_ref[c, k] = jnp.where(core == 0, up, down)


def back_near(half, me, operator, near, factor, footprint, acc, slices, margin):
    count, slots, inner, bins = near.shape
    views = slots // 2
    pixels = footprint.shape[1]
    halo = jax.ShapeDtypeStruct((2, 4, margin, pixels // 8), f32)
    return pl.pallas_call(
        back_near_kernel,
        in_specs=[SMEM, SMEM, VMEM, HBM, HBM, HBM, VMEM],
        out_specs=[VMEM] * 3,
        out_shape=[jax.ShapeDtypeStruct((slices, pixels), f32), halo, halo],
        scratch_shapes=[
            pltpu.VMEM((views, count, 2, inner, bins), f32),
            pltpu.VMEM((views, 2, count, inner, bins), f32),
            pltpu.VMEM((views, pixels, bins), bf16),
            pltpu.VMEM(acc.shape, f32),
            pltpu.SemaphoreType.DMA((views, 3)),
        ],
        compiler_params=params(52),
        cost_estimate=SMALL,
    )(half, me, operator, near, factor, footprint, acc)


def part_kernel(edge, views, staged_hbm, part_ref, sems):
    count = staged_hbm.shape[0]
    middle = count - 2 * edge
    copies = []

    def add(first, size, v, place):
        copies.append(
            pltpu.make_async_copy(
                staged_hbm.at[pl.ds(first, size), 2 * v + 1],
                part_ref.at[pl.ds(place, size)],
                sems.at[len(copies)],
            )
        )

    for v in range(views):
        add(0, edge, v, 2 * edge * v)
        add(count - edge, edge, v, 2 * edge * v + edge)
    for v in range((part_ref.shape[0] - 2 * edge * views) // middle):
        add(edge, middle, v, 2 * edge * views + middle * v)
    start_all(copies)
    for copy in copies:
        copy.wait()


def part_of(staged, edge, lasts):
    count, slots, inner, bins = staged.shape
    views = slots // 2
    part = 2 * edge * views + (count - 2 * edge) * (views - lasts)
    return pl.pallas_call(
        functools.partial(part_kernel, edge, views),
        in_specs=[HBM],
        out_specs=VMEM,
        out_shape=pltpu.VMEM((part, inner, bins), f32),
        scratch_shapes=[pltpu.SemaphoreType.DMA((3 * views,))],
        compiler_params=params(16),
        cost_estimate=SMALL,
    )(staged)


def last_kernel(edge, staged_hbm, _, last_ref, sems):
    views = staged_hbm.shape[1] // 2
    middle, lasts = last_ref.shape[:2]
    copies = [
        pltpu.make_async_copy(
            staged_hbm.at[pl.ds(edge, middle), 2 * (views - lasts + v) + 1], last_ref.at[:, v], sems.at[v]
        )
        for v in range(lasts)
    ]
    start_all(copies)
    for copy in copies:
        copy.wait()


def last_of(staged, edge, lasts, after):
    count, _, inner, bins = staged.shape
    return pl.pallas_call(
        functools.partial(last_kernel, edge),
        in_specs=[HBM, pl.BlockSpec(memory_space=pl.ANY)],
        out_specs=VMEM,
        out_shape=pltpu.VMEM((count - 2 * edge, lasts, inner, bins), f32),
        scratch_shapes=[pltpu.SemaphoreType.DMA((lasts,))],
        compiler_params=params(16),
        cost_estimate=SMALL,
    )(staged, after)


def crossing_kernel(half_ref, m_hbm, o_ref, sem):
    views, count = o_ref.shape[1], o_ref.shape[3]
    first = pl.multiple_of((1 - half_ref[0]) * count, count)
    copy = pltpu.make_async_copy(m_hbm.at[:, pl.ds(0, views), :, pl.ds(first, count)], o_ref, sem)
    copy.start()
    copy.wait()


def crossing(half, measured, views):
    segs, _, inner, slabs, bins = measured.shape
    return pl.pallas_call(
        crossing_kernel,
        in_specs=[SMEM, HBM],
        out_specs=VMEM,
        out_shape=pltpu.VMEM((segs, views, inner, slabs // 2, bins), f32),
        scratch_shapes=[pltpu.SemaphoreType.DMA],
        compiler_params=params(52),
        cost_estimate=SMALL,
    )(half, measured)


def mark_kernel(x_ref, o_ref):
    o_ref[...] = jnp.zeros_like(o_ref)


def mark(x):
    return pl.pallas_call(
        mark_kernel,
        in_specs=[pl.BlockSpec(memory_space=pl.ANY)],
        out_specs=VMEM,
        out_shape=jax.ShapeDtypeStruct((8, LANES), f32),
        compiler_params=params(16),
        cost_estimate=LARGE,
    )(x)


def back_last_kernel(half_ref, me_ref, op_ref, x_ref, factor_ref, foot_ref, in_ref, *refs):
    mine_refs, other_ref, acc_ref = refs[:4], refs[4], refs[5]
    slices, pixels = acc_ref.shape
    middle, views, inner, bins = x_ref.shape
    count = factor_ref.shape[2]
    edge = (count - middle) // 2
    far = 1 - half_ref[0]
    gap = jnp.zeros((edge * inner, bins), bf16)
    operator = op_ref[far, :slices]
    acc_ref[...] = in_ref[...]
    for v in range(views):
        weighted = ratio(factor_ref[v, far, edge : count - edge], x_ref[:, v])
        acc_ref[...] += back_project(operator, jnp.concatenate([gap, weighted, gap], axis=0), foot_ref[v])
    width = mine_refs[0].shape[1]
    for k in range(4):
        for c in range(2):
            block = me_ref[0] ^ (2 * k + c)
            part = acc_ref[:, pl.ds(pl.multiple_of(block * width, width), width)] * (1.0 / pixels)
            if c == 0:
                mine_refs[k][...] = part
            else:
                other_ref[k] = part


def back_last(half, me, operator, rows_in, factor, footprint, acc):
    slices, pixels = acc.shape
    width = pixels // 8
    return pl.pallas_call(
        back_last_kernel,
        in_specs=[SMEM, SMEM] + [VMEM] * 5,
        out_specs=[VMEM] * 5,
        out_shape=[pltpu.VMEM((slices, width), f32)] * 4 + [pltpu.VMEM((4, slices, width), f32)],
        scratch_shapes=[pltpu.VMEM((slices, pixels), f32)],
        compiler_params=params(24),
        cost_estimate=SMALL,
    )(half, me, operator, rows_in, factor, footprint, acc)


def pair_kernel(me_ref, flip_ref, *refs):
    mine_refs, theirs_ref, halo_ref, across_ref, out_refs = refs[:4], refs[4], refs[5], refs[6], refs[7:]
    core = me_ref[0] % 2
    slices, _ = mine_refs[0].shape
    margin = halo_ref.shape[2]
    for k in range(4):
        here, there = halo_ref[0, k ^ flip_ref[0]], across_ref[k ^ flip_ref[1]]
        above = jnp.where(core == 0, here, there)
        below = jnp.where(core == 0, there, here)
        out_refs[k][...] = mine_refs[k][...] + theirs_ref[k]
        out_refs[k][:margin] += above
        out_refs[k][slices - margin :] += below


def pair_sum(me, flip, mine, theirs, halo, across):
    return pl.pallas_call(
        pair_kernel,
        in_specs=[SMEM] * 2 + [VMEM] * 7,
        out_specs=[VMEM] * 4,
        out_shape=[pltpu.VMEM(x.shape, f32) for x in mine],
        compiler_params=params(16),
        cost_estimate=SMALL,
    )(me, flip, *mine, theirs, halo, across)


def assemble_kernel(me_ref, *refs):
    near_refs, far_ref, o_ref = refs[:4], refs[4], refs[5]
    width = near_refs[0].shape[1]
    for k in range(4):
        for c in range(2):
            block = me_ref[0] ^ (2 * k + c)
            part = near_refs[k][...] if c == 0 else far_ref[k]
            o_ref[:, pl.ds(pl.multiple_of(block * width, width), width)] = part


def assemble(me, near, far):
    slices, width = near[0].shape
    return pl.pallas_call(
        assemble_kernel,
        in_specs=[SMEM] + [VMEM] * 5,
        out_specs=VMEM,
        out_shape=jax.ShapeDtypeStruct((slices, width * 8), f32),
        compiler_params=params(16),
    )(me, *near, far)


def local(activity, measured, randoms, footprint, kernel, dead_counts, crystals, sensitivity):
    segs, views, inner, slabs, bins = measured.shape
    slices, pixels = activity.shape
    taps = kernel.shape[1]
    margin = (taps - 1) // 2
    width = pixels // 8
    group = lax.axis_index("seg")
    me = group.astype(jnp.int32).reshape(1)
    halves = lax.axis_size("seg") // 2

    def swap(x, k):
        return lax.ppermute(x, "seg", [(i, i ^ k) for i in range(2 * halves)])

    def shift(x, ups):
        pairs = []
        for j in range(2 * halves):
            for i in range(slabs - 1):
                source, target = (i + 1, i) if j % 2 in ups else (i, i + 1)
                to = j ^ MIRROR if i + 1 == slabs // 2 else j
                pairs.append((j * slabs + source, to * slabs + target))
        return lax.ppermute(x, ("seg", "slab"), pairs)

    count = slabs // 2
    slab = lax.axis_index("slab").astype(jnp.int32)
    half = (slab // count).reshape(1)
    edge = margin // inner
    firsts = views // 2
    lasts = 2

    def cross(x):
        return lax.ppermute(x, "slab", [(i, (i + count) % slabs) for i in range(slabs)])

    def exchange(x):
        groups = [[h * count + i for i in range(count)] for h in range(2)]
        return lax.all_to_all(x, "slab", split_axis=0, concat_axis=0, tiled=True, axis_index_groups=groups)

    ext = slices + 2 * margin
    early = cross(crossing(half, measured, firsts))
    staged = relay(half, measured, (0, 1), firsts, views - firsts, count)
    staged, near_activity = lax.optimization_barrier((staged, activity))
    staged = exchange(staged)
    near = relay(half, measured, (0,), 0, firsts, count, slots=2, cost=SMALL)
    efficiency, operator, operator_t = setup(me, kernel, dead_counts, crystals, slices, segs, inner, halves)
    even = group % 2 == 0
    above = shift(near_activity[slices - margin :], ())
    below = shift(near_activity[:margin], (0, 1))
    staged, near, begun, efficiency, operator, operator_t, above, below = lax.optimization_barrier(
        (staged, near, mark(early), efficiency, operator, operator_t, above, below)
    )
    part = cross(part_of(staged, edge, lasts))
    near = relay(half, early, (1,), 0, firsts, count, into=near, slot=1, slots=2, after=[begun])
    rows_last = cross(last_of(staged, edge, lasts, near))
    near = exchange(near)
    factor = forward(operator, activity, above, below, footprint, randoms, efficiency)

    acc, last_factor, last_foot = back_staged(
        half, operator_t, staged, part, factor, footprint, edge, lasts
    )
    acc, keep, give = back_near(half, me, operator_t, near, factor, footprint, acc, slices, margin)
    halo = shift(keep + swap(give, 1)[::-1], (1,))
    across = swap(halo[1], 1)
    *mine, other = back_last(half, me, operator_t, rows_last, last_factor, last_foot, acc)
    sides = [jnp.where(even, slab == count, slab == count - 1), jnp.where(even, slab == count - 1, slab == count)]
    flip = jnp.where(jnp.stack(sides), MIRROR // 2, 0).astype(jnp.int32)
    pair = pair_sum(me, flip, mine, swap(other, 1), halo, across)
    total = pair[0]
    for k in range(1, 4):
        total = total + swap(pair[k], 2 * k)
    start = group * width
    gain = lax.dynamic_slice_in_dim(activity, start, width, 1) / lax.dynamic_slice_in_dim(
        sensitivity, start, width, 1
    )
    block = total * gain
    near = [block] + [swap(block, 2 * k) for k in range(1, 4)]
    far = swap(jnp.stack(near), 1)
    return assemble(me, near, far)


def solution(mesh):
    placed = (
        P("slab", None),
        P("seg", None, "slab", None, None),
        P("seg", None, "slab", None),
        P(),
        P(),
        P(),
        P(),
        P("slab", None),
    )
    return jax.shard_map(
        local, mesh=mesh, in_specs=placed, out_specs=P("slab", None), check_vma=False
    )
```

```python
import functools
import jax
import jax.numpy as jnp
from jax import lax
from jax.experimental import pallas as pl
from jax.experimental.pallas import tpu as pltpu
from jax.sharding import PartitionSpec as P

dead_time_tau = 0.001
f32 = jnp.float32
bf16 = jnp.bfloat16
LANES = 128
MIRROR = 6
LASTS = 4
VMEM = pl.BlockSpec(memory_space=pltpu.VMEM)
SMEM = pl.BlockSpec(memory_space=pltpu.SMEM)
HBM = pl.BlockSpec(memory_space=pltpu.HBM)
SMALL = pl.CostEstimate(flops=1, bytes_accessed=1, transcendentals=0)
LARGE = pl.CostEstimate(flops=10**12, bytes_accessed=1 << 20, transcendentals=0)


def params(mib):
    return pltpu.CompilerParams(vmem_limit_bytes=mib << 20)


def lane_blocks(bins):
    return bins // LANES


def relay_kernel(sides, lanes, half_ref, *refs):
    m_refs, o_ref = refs[:lanes], refs[-1]
    segs, _, inner, slabs, _ = m_refs[0].shape
    rows = segs * inner
    count = o_ref.shape[0]
    for lane, m_ref in enumerate(m_refs):
        flat = m_ref.reshape(rows * slabs, LANES)
        cols = slice(lane * LANES, (lane + 1) * LANES)
        for slot, side in enumerate(sides):
            first = 0 if slabs == count else (half_ref[0] ^ side) * count
            for s in range(count):
                o_ref[s, slot, :, cols] = flat[pl.ds(first + s, rows, stride=slabs), :]


def relay(half, measured, sides, first_view, views, count, slots, into=None, slot=0, step=1, after=()):
    segs, _, inner, slabs, bins = measured.shape
    rows = segs * inner
    specs = [
        pl.BlockSpec((segs, 1, inner, slabs, LANES), lambda v, lane=lane: (0, first_view + v, 0, 0, lane))
        for lane in range(lane_blocks(bins))
    ]
    lanes = len(specs)
    operands = [half] + [measured] * lanes
    aliases = {}
    if into is not None:
        aliases = {len(operands): 0}
        operands.append(into)
    operands += after
    specs = [SMEM] + specs + [pl.BlockSpec(memory_space=pl.ANY)] * (len(operands) - 1 - lanes)
    return pl.pallas_call(
        functools.partial(relay_kernel, sides, lanes),
        grid=(views,),
        in_specs=specs,
        out_specs=pl.BlockSpec((count, len(sides), rows, bins), lambda v: (0, slot + step * v, 0, 0)),
        out_shape=jax.ShapeDtypeStruct((count, slots, rows, bins), f32),
        input_output_aliases=aliases,
        compiler_params=params(52),
        cost_estimate=SMALL,
    )(*operands)


def split_two(x):
    hi = x.astype(bf16)
    return hi, (x - hi.astype(f32)).astype(bf16)


def axial_entries(weight, slices, margin, segs, inner, row, column):
    place = jnp.where(
        column < slices, column + margin, jnp.where(column < slices + margin, column - slices, column)
    )
    group = (row // inner) % segs
    tap = place - (row // (inner * segs) * inner + row % inner)
    entries = jnp.zeros(row.shape, f32)
    for k in range(2 * margin + 1):
        value = jnp.full(row.shape, weight(0, k), f32)
        for g in range(1, segs):
            value = jnp.where(group == g, weight(g, k), value)
        entries = jnp.where(tap == k, value, entries)
    return entries


def setup_kernel(slices, segs, inner, halves, me_ref, k_ref, t_ref, c_ref, o_ref, op_ref, opt_ref):
    lanes, depth = t_ref.shape
    views = o_ref.shape[0]
    bins = c_ref.shape[-1]
    taps = k_ref.shape[1]
    margin = (taps - 1) // 2
    first_row = me_ref[0] % halves * segs
    turned = me_ref[0] >= halves

    def weight(g, k):
        return jnp.where(turned, k_ref[first_row + g, taps - 1 - k], k_ref[first_row + g, k])

    def ids(shape, dim):
        return lax.broadcasted_iota(jnp.int32, shape, dim)

    shape = op_ref.shape
    op_ref[...] = axial_entries(weight, slices, margin, segs, inner, ids(shape, 0), ids(shape, 1))
    _, ext, part = opt_ref.shape
    for h in range(2):
        opt_ref[h] = axial_entries(
            weight, slices, margin, segs, inner, ids((ext, part), 1) + h * part, ids((ext, part), 0)
        )

    table = t_ref[...].astype(f32)
    first = table.astype(bf16)
    rest = table - first.astype(f32)
    second = rest.astype(bf16)
    third = (rest - second.astype(f32)).astype(bf16)
    pieces = jnp.concatenate([first, second, third], axis=0)
    depth_ids = ids((depth, bins), 0)
    lane_ids = ids((lanes, bins), 0)

    def look(index):
        row = index // lanes
        hot = jnp.where(depth_ids == row, 1.0, 0.0).astype(bf16)
        got = jnp.dot(pieces, hot, preferred_element_type=f32)
        value = got[:lanes] + got[lanes : 2 * lanes] + got[2 * lanes :]
        return jnp.sum(jnp.where(lane_ids == index - row * lanes, value, 0.0), axis=0, keepdims=True)

    def one_view(v, carry):
        first_factor = 1.0 + dead_time_tau * look(c_ref[0, v])
        second_factor = 1.0 + dead_time_tau * look(c_ref[1, v])
        o_ref[v] = 1.0 / (first_factor * second_factor)
        return carry

    lax.fori_loop(0, views, one_view, 0)


def setup(me, kernel, dead_counts, crystals, slices, segs, inner, halves):
    _, views, bins = crystals.shape
    taps = kernel.shape[1]
    rows = slices * segs
    ext = slices + taps - 1 + 8
    table = dead_counts.reshape(-1, LANES).T
    return pl.pallas_call(
        functools.partial(setup_kernel, slices, segs, inner, halves),
        in_specs=[SMEM, SMEM, VMEM, VMEM],
        out_specs=[VMEM] * 3,
        out_shape=[
            jax.ShapeDtypeStruct((views, 1, bins), f32),
            jax.ShapeDtypeStruct((rows, ext), f32),
            jax.ShapeDtypeStruct((2, ext, rows // 2), f32),
        ],
        compiler_params=params(24),
        cost_estimate=SMALL,
    )(me, kernel, table, crystals.reshape(2, views, 1, bins))


def forward_kernel(op_ref, act_ref, above_ref, below_ref, foot_hbm, eff_ref, *refs):
    lanes = (len(refs) - 5) // 2
    rand_refs, o_ref, foot_ref, rows_ref = refs[:lanes], refs[lanes], refs[lanes + 1], refs[lanes + 2]
    order_refs, ext_ref, sems = refs[lanes + 3 : -2], refs[-2], refs[-1]
    segs, _, slices, _ = rand_refs[0].shape
    pixels = ext_ref.shape[1]
    margin = above_ref.shape[0]
    inner = 2
    count = slices // inner
    view = pl.program_id(0)

    def fetch(v):
        return pltpu.make_async_copy(foot_hbm.at[v], foot_ref.at[v], sems.at[v])

    @pl.when(view == 0)
    def _():
        for v in range(foot_ref.shape[0]):
            fetch(v).start()
        ext_ref[...] = jnp.zeros_like(ext_ref)
        ext_ref[:slices] = act_ref[...]
        ext_ref[slices : slices + margin] = above_ref[...]
        ext_ref[slices + margin : slices + 2 * margin] = below_ref[...]
        rows_ref[...] = jnp.dot(
            op_ref[...], ext_ref[...], preferred_element_type=f32, precision=lax.Precision.HIGHEST
        ).astype(bf16)

    fetch(view).wait()
    projected = jnp.dot(rows_ref[...], foot_ref[view], preferred_element_type=f32) * (1.0 / pixels)
    for lane in range(lanes):
        flat = rand_refs[lane].reshape(segs * slices, LANES)
        order_ref = order_refs[lane]
        for g in range(segs):
            for a in range(inner):
                got = flat[pl.ds(g * slices + a, count, stride=inner), :].astype(f32)
                order_ref[pl.ds(g * inner + a, count, stride=segs * inner), :] = 0.25 * (got + 1.0)
        cols = slice(lane * LANES, (lane + 1) * LANES)
        eff = eff_ref[0, :, cols]
        value = eff / (eff * projected[:, cols] + order_ref[...])
        o_ref[0, :, :, :, cols] = value.reshape(*o_ref.shape[1:4], LANES)


def forward(operator, activity, above, below, footprint, randoms, efficiency):
    segs, views, slices, bins = randoms.shape
    pixels = footprint.shape[1]
    rows = segs * slices
    inner = 2 * segs
    lanes = [
        pl.BlockSpec((segs, 1, slices, LANES), lambda v, lane=lane: (0, v, 0, lane))
        for lane in range(lane_blocks(bins))
    ]
    return pl.pallas_call(
        forward_kernel,
        grid=(views,),
        in_specs=[
            VMEM,
            VMEM,
            VMEM,
            VMEM,
            HBM,
            pl.BlockSpec((1, 1, bins), lambda v: (v, 0, 0)),
        ]
        + lanes,
        out_specs=pl.BlockSpec((1, 2, rows // inner // 2, inner, bins), lambda v: (v, 0, 0, 0, 0)),
        out_shape=pltpu.HBM((views, 2, rows // inner // 2, inner, bins), f32),
        scratch_shapes=[pltpu.VMEM(footprint.shape, footprint.dtype), pltpu.VMEM((rows, pixels), bf16)]
        + [pltpu.VMEM((rows, LANES), f32)] * len(lanes)
        + [pltpu.VMEM((operator.shape[1], pixels), f32), pltpu.SemaphoreType.DMA((views,))],
        compiler_params=params(40),
        cost_estimate=SMALL,
    )(operator, activity, above, below, footprint, efficiency, *[randoms] * len(lanes))


def back_project(operator, weighted, foot):
    ext = operator.shape[0]
    hi, lo = split_two(operator)
    both = jnp.dot(jnp.concatenate([hi, lo], axis=0), weighted, preferred_element_type=f32)
    hi, lo = split_two(both[:ext] + both[ext:])
    spread = lax.dot_general(
        jnp.concatenate([hi, lo], axis=0), foot, (((1,), (1,)), ((), ())), preferred_element_type=f32
    )
    return spread[:ext] + spread[ext:]


def ratio(factor, rows_in):
    scaled = factor * rows_in
    return scaled.reshape(-1, scaled.shape[-1]).astype(bf16)


def start_all(copies):
    for copy in copies:
        copy.start()


def back_staged_kernel(
    edge,
    half_ref,
    op_ref,
    staged_hbm,
    part_ref,
    factor_hbm,
    foot_hbm,
    acc_ref,
    own_ref,
    factor_ref,
    foot_ref,
    sems,
):
    half = half_ref[0]
    views, _, count, inner, bins = factor_ref.shape
    bare = views - own_ref.shape[0]
    firsts = factor_hbm.shape[0] - views
    middles = (part_ref.shape[0] - 2 * edge * views) // (count - 2 * edge)

    def copies(v):
        own = []
        if v >= bare:
            slot = bare + 2 * (v - bare)
            own = [pltpu.make_async_copy(staged_hbm.at[:, slot], own_ref.at[v - bare], sems.at[v, 0])]
        return own + [
            pltpu.make_async_copy(factor_hbm.at[firsts + v], factor_ref.at[v], sems.at[v, 1]),
            pltpu.make_async_copy(foot_hbm.at[firsts + v], foot_ref.at[v], sems.at[v, 2]),
        ]

    for v in range(views):
        start_all(copies(v))
    operator = jnp.concatenate([op_ref[half], op_ref[1 - half]], axis=1)
    for v in range(views):
        for copy in copies(v):
            copy.wait()
        far = factor_ref[v, 1 - half]
        if v >= bare:
            own = ratio(factor_ref[v, half], own_ref[v - bare])
        else:
            own = jnp.zeros((count * inner, bins), bf16)
        low = ratio(far[:edge], part_ref[2 * edge * v : 2 * edge * v + edge])
        high = ratio(far[count - edge :], part_ref[2 * edge * v + edge : 2 * edge * (v + 1)])
        if v < middles:
            first = 2 * edge * views + (count - 2 * edge) * v
            middle = ratio(far[edge : count - edge], part_ref[first : first + count - 2 * edge])
        else:
            middle = jnp.zeros(((count - 2 * edge) * inner, bins), bf16)
        spread = back_project(operator, jnp.concatenate([own, low, middle, high], axis=0), foot_ref[v])
        if v == 0:
            acc_ref[...] = spread
        else:
            acc_ref[...] += spread


def back_staged(half, operator, staged, part, factor, footprint, edge, views):
    ext = operator.shape[1]
    count, slots, inner, bins = staged.shape
    pixels = footprint.shape[1]
    return pl.pallas_call(
        functools.partial(back_staged_kernel, edge),
        in_specs=[SMEM, VMEM, HBM, VMEM, HBM, HBM],
        out_specs=VMEM,
        out_shape=pltpu.VMEM((ext, pixels), f32),
        scratch_shapes=[
            pltpu.VMEM((slots - views, count, inner, bins), f32),
            pltpu.VMEM((views, 2, count, inner, bins), f32),
            pltpu.VMEM((views, pixels, bins), bf16),
            pltpu.SemaphoreType.DMA((views, 3)),
        ],
        compiler_params=params(52),
        cost_estimate=LARGE,
    )(half, operator, staged, part, factor, footprint)


def back_near_kernel(
    half_ref, me_ref, op_ref, near_hbm, factor_hbm, foot_hbm, in_ref, acc_ref, keep_ref, give_ref, *scratch
):
    near_ref, factor_ref, foot_ref, sum_ref, sems = scratch
    half = half_ref[0]
    views = factor_ref.shape[0]
    firsts = near_hbm.shape[1] - views

    def copies(v):
        slot, size = (2 * v, 2) if v < firsts else (firsts + v, 1)
        return [
            pltpu.make_async_copy(
                near_hbm.at[:, pl.ds(slot, size)], near_ref.at[:, pl.ds(slot, size)], sems.at[v, 0]
            ),
            pltpu.make_async_copy(factor_hbm.at[v], factor_ref.at[v], sems.at[v, 1]),
            pltpu.make_async_copy(foot_hbm.at[v], foot_ref.at[v], sems.at[v, 2]),
        ]

    for v in range(views):
        start_all(copies(v))
    operator = jnp.concatenate([op_ref[half], op_ref[1 - half]], axis=1)
    sum_ref[...] = in_ref[...]
    for v in range(views):
        for copy in copies(v):
            copy.wait()
        if v < firsts:
            own = ratio(factor_ref[v, half], near_ref[:, 2 * v])
            far = ratio(factor_ref[v, 1 - half], near_ref[:, 2 * v + 1])
        else:
            own = ratio(factor_ref[v, half], near_ref[:, firsts + v])
            far = jnp.zeros_like(own)
        sum_ref[...] += back_project(operator, jnp.concatenate([own, far], axis=0), foot_ref[v])
    slices, pixels = acc_ref.shape
    margin, width = keep_ref.shape[2:]
    acc_ref[...] = sum_ref[:slices]
    core = me_ref[0] % 2
    for k in range(4):
        for c in range(2):
            block = me_ref[0] ^ (2 * k + c)
            cols = pl.ds(pl.multiple_of(block * width, width), width)
            pair = sum_ref[slices : slices + 2 * margin, cols] * (1.0 / pixels)
            up, down = pair[:margin], pair[margin:]
            keep_ref[c, k] = jnp.where(core == 0, down, up)
            give_ref[c, k] = jnp.where(core == 0, up, down)


def back_near(half, me, operator, near, factor, footprint, acc, slices, margin, views):
    count, slots, inner, bins = near.shape
    pixels = footprint.shape[1]
    halo = jax.ShapeDtypeStruct((2, 4, margin, pixels // 8), f32)
    return pl.pallas_call(
        back_near_kernel,
        in_specs=[SMEM, SMEM, VMEM, HBM, HBM, HBM, VMEM],
        out_specs=[VMEM] * 3,
        out_shape=[jax.ShapeDtypeStruct((slices, pixels), f32), halo, halo],
        scratch_shapes=[
            pltpu.VMEM((count, slots, inner, bins), f32),
            pltpu.VMEM((views, 2, count, inner, bins), f32),
            pltpu.VMEM((views, pixels, bins), bf16),
            pltpu.VMEM(acc.shape, f32),
            pltpu.SemaphoreType.DMA((views, 3)),
        ],
        compiler_params=params(52),
        cost_estimate=SMALL,
    )(half, me, operator, near, factor, footprint, acc)


def far_slot(v, views, slots):
    bare = 2 * views - slots
    return v if v < bare else bare + 2 * (v - bare) + 1


def part_kernel(edge, views, staged_hbm, part_ref, sems):
    count, slots = staged_hbm.shape[:2]
    middle = count - 2 * edge
    copies = []

    def add(first, size, v, place):
        copies.append(
            pltpu.make_async_copy(
                staged_hbm.at[pl.ds(first, size), far_slot(v, views, slots)],
                part_ref.at[pl.ds(place, size)],
                sems.at[len(copies)],
            )
        )

    for v in range(views):
        add(0, edge, v, 2 * edge * v)
        add(count - edge, edge, v, 2 * edge * v + edge)
    for v in range((part_ref.shape[0] - 2 * edge * views) // middle):
        add(edge, middle, v, 2 * edge * views + middle * v)
    start_all(copies)
    for copy in copies:
        copy.wait()


def part_of(staged, edge, views, lasts):
    count, slots, inner, bins = staged.shape
    part = 2 * edge * views + (count - 2 * edge) * (views - lasts)
    return pl.pallas_call(
        functools.partial(part_kernel, edge, views),
        in_specs=[HBM],
        out_specs=VMEM,
        out_shape=pltpu.VMEM((part, inner, bins), f32),
        scratch_shapes=[pltpu.SemaphoreType.DMA((3 * views,))],
        compiler_params=params(16),
        cost_estimate=SMALL,
    )(staged)


def last_kernel(edge, views, staged_hbm, _, last_ref, sems):
    slots = staged_hbm.shape[1]
    middle, lasts = last_ref.shape[:2]
    copies = [
        pltpu.make_async_copy(
            staged_hbm.at[pl.ds(edge, middle), far_slot(views - lasts + v, views, slots)],
            last_ref.at[:, v],
            sems.at[v],
        )
        for v in range(lasts)
    ]
    start_all(copies)
    for copy in copies:
        copy.wait()


def last_of(staged, edge, views, lasts, after):
    count, _, inner, bins = staged.shape
    return pl.pallas_call(
        functools.partial(last_kernel, edge, views),
        in_specs=[HBM, pl.BlockSpec(memory_space=pl.ANY)],
        out_specs=VMEM,
        out_shape=pltpu.VMEM((count - 2 * edge, lasts, inner, bins), f32),
        scratch_shapes=[pltpu.SemaphoreType.DMA((lasts,))],
        compiler_params=params(16),
        cost_estimate=SMALL,
    )(staged, after)


def crossing_kernel(half_ref, m_hbm, o_ref, sem):
    views, count = o_ref.shape[1], o_ref.shape[3]
    first = pl.multiple_of((1 - half_ref[0]) * count, count)
    copy = pltpu.make_async_copy(m_hbm.at[:, pl.ds(0, views), :, pl.ds(first, count)], o_ref, sem)
    copy.start()
    copy.wait()


def crossing(half, measured, views):
    segs, _, inner, slabs, bins = measured.shape
    return pl.pallas_call(
        crossing_kernel,
        in_specs=[SMEM, HBM],
        out_specs=VMEM,
        out_shape=pltpu.VMEM((segs, views, inner, slabs // 2, bins), f32),
        scratch_shapes=[pltpu.SemaphoreType.DMA],
        compiler_params=params(52),
        cost_estimate=SMALL,
    )(half, measured)


def mark_kernel(x_ref, o_ref):
    o_ref[...] = jnp.zeros_like(o_ref)


def mark(x):
    return pl.pallas_call(
        mark_kernel,
        in_specs=[pl.BlockSpec(memory_space=pl.ANY)],
        out_specs=VMEM,
        out_shape=jax.ShapeDtypeStruct((8, LANES), f32),
        compiler_params=params(16),
        cost_estimate=LARGE,
    )(x)


def back_last_kernel(half_ref, me_ref, op_ref, x_ref, factor_hbm, foot_hbm, in_ref, *refs):
    mine_refs, (other_ref, acc_ref, factor_ref, foot_ref, sems) = refs[:4], refs[4:]
    slices, pixels = acc_ref.shape
    middle, views, inner, bins = x_ref.shape
    count = factor_ref.shape[1]
    edge = (count - middle) // 2
    far = 1 - half_ref[0]
    first = factor_hbm.shape[0] - views

    def copies(v):
        return [
            pltpu.make_async_copy(factor_hbm.at[first + v, far], factor_ref.at[v], sems.at[v, 0]),
            pltpu.make_async_copy(foot_hbm.at[first + v], foot_ref.at[v], sems.at[v, 1]),
        ]

    for v in range(views):
        start_all(copies(v))
    gap = jnp.zeros((edge * inner, bins), bf16)
    operator = op_ref[far, :slices]
    acc_ref[...] = in_ref[...]
    for v in range(views):
        for copy in copies(v):
            copy.wait()
        weighted = ratio(factor_ref[v, edge : count - edge], x_ref[:, v])
        acc_ref[...] += back_project(operator, jnp.concatenate([gap, weighted, gap], axis=0), foot_ref[v])
    width = mine_refs[0].shape[1]
    for k in range(4):
        for c in range(2):
            block = me_ref[0] ^ (2 * k + c)
            part = acc_ref[:, pl.ds(pl.multiple_of(block * width, width), width)] * (1.0 / pixels)
            if c == 0:
                mine_refs[k][...] = part
            else:
                other_ref[k] = part


def back_last(half, me, operator, rows_in, factor, footprint, acc):
    slices, pixels = acc.shape
    width = pixels // 8
    _, views, inner, bins = rows_in.shape
    return pl.pallas_call(
        back_last_kernel,
        in_specs=[SMEM, SMEM, VMEM, VMEM, HBM, HBM, VMEM],
        out_specs=[VMEM] * 5,
        out_shape=[pltpu.VMEM((slices, width), f32)] * 4 + [pltpu.VMEM((4, slices, width), f32)],
        scratch_shapes=[
            pltpu.VMEM((slices, pixels), f32),
            pltpu.VMEM((views, factor.shape[2], inner, bins), f32),
            pltpu.VMEM((views, pixels, bins), bf16),
            pltpu.SemaphoreType.DMA((views, 2)),
        ],
        compiler_params=params(52),
        cost_estimate=SMALL,
    )(half, me, operator, rows_in, factor, footprint, acc)


def pair_kernel(me_ref, flip_ref, *refs):
    mine_refs, theirs_ref, halo_ref, across_ref, out_refs = refs[:4], refs[4], refs[5], refs[6], refs[7:]
    core = me_ref[0] % 2
    slices, _ = mine_refs[0].shape
    margin = halo_ref.shape[2]
    for k in range(4):
        here, there = halo_ref[0, k ^ flip_ref[0]], across_ref[k ^ flip_ref[1]]
        above = jnp.where(core == 0, here, there)
        below = jnp.where(core == 0, there, here)
        out_refs[k][...] = mine_refs[k][...] + theirs_ref[k]
        out_refs[k][:margin] += above
        out_refs[k][slices - margin :] += below


def pair_sum(me, flip, mine, theirs, halo, across):
    return pl.pallas_call(
        pair_kernel,
        in_specs=[SMEM] * 2 + [VMEM] * 7,
        out_specs=[VMEM] * 4,
        out_shape=[pltpu.VMEM(x.shape, f32) for x in mine],
        compiler_params=params(16),
        cost_estimate=SMALL,
    )(me, flip, *mine, theirs, halo, across)


def assemble_kernel(me_ref, *refs):
    near_refs, far_ref, o_ref = refs[:4], refs[4], refs[5]
    width = near_refs[0].shape[1]
    for k in range(4):
        for c in range(2):
            block = me_ref[0] ^ (2 * k + c)
            part = near_refs[k][...] if c == 0 else far_ref[k]
            o_ref[:, pl.ds(pl.multiple_of(block * width, width), width)] = part


def assemble(me, near, far):
    slices, width = near[0].shape
    return pl.pallas_call(
        assemble_kernel,
        in_specs=[SMEM] + [VMEM] * 5,
        out_specs=VMEM,
        out_shape=jax.ShapeDtypeStruct((slices, width * 8), f32),
        compiler_params=params(16),
    )(me, *near, far)


def local(activity, measured, randoms, footprint, kernel, dead_counts, crystals, sensitivity):
    segs, views, inner, slabs, bins = measured.shape
    slices, pixels = activity.shape
    taps = kernel.shape[1]
    margin = (taps - 1) // 2
    width = pixels // 8
    group = lax.axis_index("seg")
    me = group.astype(jnp.int32).reshape(1)
    halves = lax.axis_size("seg") // 2

    def swap(x, k):
        return lax.ppermute(x, "seg", [(i, i ^ k) for i in range(2 * halves)])

    def shift(x, ups):
        pairs = []
        for j in range(2 * halves):
            for i in range(slabs - 1):
                source, target = (i + 1, i) if j % 2 in ups else (i, i + 1)
                to = j ^ MIRROR if i + 1 == slabs // 2 else j
                pairs.append((j * slabs + source, to * slabs + target))
        return lax.ppermute(x, ("seg", "slab"), pairs)

    count = slabs // 2
    slab = lax.axis_index("slab").astype(jnp.int32)
    half = (slab // count).reshape(1)
    edge = margin // inner
    firsts, bare, lasts = 3, 2, LASTS
    behind = views - firsts

    def cross(x):
        return lax.ppermute(x, "slab", [(i, (i + count) % slabs) for i in range(slabs)])

    def exchange(x):
        groups = [[h * count + i for i in range(count)] for h in range(2)]
        return lax.all_to_all(x, "slab", split_axis=0, concat_axis=0, tiled=True, axis_index_groups=groups)

    ext = slices + 2 * margin
    early = cross(crossing(half, measured, firsts))
    staged = relay(half, measured, (1,), firsts, bare, count, 2 * behind - bare)
    staged = relay(
        half, measured, (0, 1), firsts + bare, behind - bare, count, 2 * behind - bare, into=staged, slot=bare // 2
    )
    staged, near_activity = lax.optimization_barrier((staged, activity))
    staged = exchange(staged)
    near = relay(half, measured, (0,), 0, firsts, count, 2 * firsts + bare, step=2)
    near = relay(half, measured, (0,), firsts, bare, count, 2 * firsts + bare, into=near, slot=2 * firsts)
    efficiency, operator, operator_t = setup(me, kernel, dead_counts, crystals, slices, segs, inner, halves)
    even = group % 2 == 0
    above = shift(near_activity[slices - margin :], ())
    below = shift(near_activity[:margin], (0, 1))
    staged, near, begun, efficiency, operator, operator_t, above, below = lax.optimization_barrier(
        (staged, near, mark(early), efficiency, operator, operator_t, above, below)
    )
    part = cross(part_of(staged, edge, behind, lasts))
    near = relay(
        half, early, (1,), 0, firsts, count, 2 * firsts + bare, into=near, slot=1, step=2, after=[begun]
    )
    rows_last = cross(last_of(staged, edge, behind, lasts, near))
    near = exchange(near)
    factor = forward(operator, activity, above, below, footprint, randoms, efficiency)

    acc = back_staged(half, operator_t, staged, part, factor, footprint, edge, behind)
    acc, keep, give = back_near(half, me, operator_t, near, factor, footprint, acc, slices, margin, firsts + bare)
    halo = shift(keep + swap(give, 1)[::-1], (1,))
    across = swap(halo[1], 1)
    *mine, other = back_last(half, me, operator_t, rows_last, factor, footprint, acc)
    sides = [jnp.where(even, slab == count, slab == count - 1), jnp.where(even, slab == count - 1, slab == count)]
    flip = jnp.where(jnp.stack(sides), MIRROR // 2, 0).astype(jnp.int32)
    pair = pair_sum(me, flip, mine, swap(other, 1), halo, across)
    total = pair[0]
    for k in range(1, 4):
        total = total + swap(pair[k], 2 * k)
    start = group * width
    gain = lax.dynamic_slice_in_dim(activity, start, width, 1) / lax.dynamic_slice_in_dim(
        sensitivity, start, width, 1
    )
    block = total * gain
    near = [block] + [swap(block, 2 * k) for k in range(1, 4)]
    far = swap(jnp.stack(near), 1)
    return assemble(me, near, far)


def solution(mesh):
    placed = (
        P("slab", None),
        P("seg", None, "slab", None, None),
        P("seg", None, "slab", None),
        P(),
        P(),
        P(),
        P(),
        P("slab", None),
    )
    return jax.shard_map(
        local, mesh=mesh, in_specs=placed, out_specs=P("slab", None), check_vma=False
    )
```

```python
import functools
import jax
import jax.numpy as jnp
from jax import lax
from jax.experimental import pallas as pl
from jax.experimental.pallas import tpu as pltpu
from jax.sharding import PartitionSpec as P

dead_time_tau = 0.001
f32 = jnp.float32
bf16 = jnp.bfloat16
LANES = 128
MIRROR = 6
LASTS = 5
VMEM = pl.BlockSpec(memory_space=pltpu.VMEM)
SMEM = pl.BlockSpec(memory_space=pltpu.SMEM)
HBM = pl.BlockSpec(memory_space=pltpu.HBM)
SMALL = pl.CostEstimate(flops=1, bytes_accessed=1, transcendentals=0)
LARGE = pl.CostEstimate(flops=10**12, bytes_accessed=1 << 20, transcendentals=0)


def params(mib):
    return pltpu.CompilerParams(vmem_limit_bytes=mib << 20)


def lane_blocks(bins):
    return bins // LANES


def relay_kernel(sides, lanes, half_ref, *refs):
    m_refs, o_ref = refs[:lanes], refs[-1]
    segs, _, inner, slabs, _ = m_refs[0].shape
    rows = segs * inner
    count = o_ref.shape[0]
    for lane, m_ref in enumerate(m_refs):
        flat = m_ref.reshape(rows * slabs, LANES)
        cols = slice(lane * LANES, (lane + 1) * LANES)
        for slot, side in enumerate(sides):
            first = 0 if slabs == count else (half_ref[0] ^ side) * count
            for s in range(count):
                o_ref[s, slot, :, cols] = flat[pl.ds(first + s, rows, stride=slabs), :]


def relay(half, measured, sides, first_view, views, count, slots, into=None, slot=0, step=1, after=()):
    segs, _, inner, slabs, bins = measured.shape
    rows = segs * inner
    specs = [
        pl.BlockSpec((segs, 1, inner, slabs, LANES), lambda v, lane=lane: (0, first_view + v, 0, 0, lane))
        for lane in range(lane_blocks(bins))
    ]
    lanes = len(specs)
    operands = [half] + [measured] * lanes
    aliases = {}
    if into is not None:
        aliases = {len(operands): 0}
        operands.append(into)
    operands += after
    specs = [SMEM] + specs + [pl.BlockSpec(memory_space=pl.ANY)] * (len(operands) - 1 - lanes)
    return pl.pallas_call(
        functools.partial(relay_kernel, sides, lanes),
        grid=(views,),
        in_specs=specs,
        out_specs=pl.BlockSpec((count, len(sides), rows, bins), lambda v: (0, slot + step * v, 0, 0)),
        out_shape=jax.ShapeDtypeStruct((count, slots, rows, bins), f32),
        input_output_aliases=aliases,
        compiler_params=params(52),
        cost_estimate=SMALL,
    )(*operands)


def split_two(x):
    hi = x.astype(bf16)
    return hi, (x - hi.astype(f32)).astype(bf16)


def axial_entries(weight, slices, margin, segs, inner, row, column):
    place = jnp.where(
        column < slices, column + margin, jnp.where(column < slices + margin, column - slices, column)
    )
    group = (row // inner) % segs
    tap = place - (row // (inner * segs) * inner + row % inner)
    entries = jnp.zeros(row.shape, f32)
    for k in range(2 * margin + 1):
        value = jnp.full(row.shape, weight(0, k), f32)
        for g in range(1, segs):
            value = jnp.where(group == g, weight(g, k), value)
        entries = jnp.where(tap == k, value, entries)
    return entries


def setup_kernel(slices, segs, inner, halves, me_ref, k_ref, t_ref, c_ref, o_ref, op_ref, opt_ref):
    lanes, depth = t_ref.shape
    views = o_ref.shape[0]
    bins = c_ref.shape[-1]
    taps = k_ref.shape[1]
    margin = (taps - 1) // 2
    first_row = me_ref[0] % halves * segs
    turned = me_ref[0] >= halves

    def weight(g, k):
        return jnp.where(turned, k_ref[first_row + g, taps - 1 - k], k_ref[first_row + g, k])

    def ids(shape, dim):
        return lax.broadcasted_iota(jnp.int32, shape, dim)

    shape = op_ref.shape
    op_ref[...] = axial_entries(weight, slices, margin, segs, inner, ids(shape, 0), ids(shape, 1))
    _, ext, part = opt_ref.shape
    for h in range(2):
        opt_ref[h] = axial_entries(
            weight, slices, margin, segs, inner, ids((ext, part), 1) + h * part, ids((ext, part), 0)
        )

    table = t_ref[...].astype(f32)
    first = table.astype(bf16)
    rest = table - first.astype(f32)
    second = rest.astype(bf16)
    third = (rest - second.astype(f32)).astype(bf16)
    pieces = jnp.concatenate([first, second, third], axis=0)
    depth_ids = ids((depth, bins), 0)
    lane_ids = ids((lanes, bins), 0)

    def look(index):
        row = index // lanes
        hot = jnp.where(depth_ids == row, 1.0, 0.0).astype(bf16)
        got = jnp.dot(pieces, hot, preferred_element_type=f32)
        value = got[:lanes] + got[lanes : 2 * lanes] + got[2 * lanes :]
        return jnp.sum(jnp.where(lane_ids == index - row * lanes, value, 0.0), axis=0, keepdims=True)

    def one_view(v, carry):
        first_factor = 1.0 + dead_time_tau * look(c_ref[0, v])
        second_factor = 1.0 + dead_time_tau * look(c_ref[1, v])
        o_ref[v] = 1.0 / (first_factor * second_factor)
        return carry

    lax.fori_loop(0, views, one_view, 0)


def setup(me, kernel, dead_counts, crystals, slices, segs, inner, halves):
    _, views, bins = crystals.shape
    taps = kernel.shape[1]
    rows = slices * segs
    ext = slices + taps - 1 + 8
    table = dead_counts.reshape(-1, LANES).T
    return pl.pallas_call(
        functools.partial(setup_kernel, slices, segs, inner, halves),
        in_specs=[SMEM, SMEM, VMEM, VMEM],
        out_specs=[VMEM] * 3,
        out_shape=[
            jax.ShapeDtypeStruct((views, 1, bins), f32),
            jax.ShapeDtypeStruct((rows, ext), f32),
            jax.ShapeDtypeStruct((2, ext, rows // 2), f32),
        ],
        compiler_params=params(24),
        cost_estimate=SMALL,
    )(me, kernel, table, crystals.reshape(2, views, 1, bins))


def forward_kernel(op_ref, act_ref, above_ref, below_ref, foot_hbm, eff_ref, *refs):
    lanes = (len(refs) - 5) // 2
    rand_refs, o_ref, foot_ref, rows_ref = refs[:lanes], refs[lanes], refs[lanes + 1], refs[lanes + 2]
    order_refs, ext_ref, sems = refs[lanes + 3 : -2], refs[-2], refs[-1]
    segs, _, slices, _ = rand_refs[0].shape
    pixels = ext_ref.shape[1]
    margin = above_ref.shape[0]
    inner = 2
    count = slices // inner
    view = pl.program_id(0)

    def fetch(v):
        return pltpu.make_async_copy(foot_hbm.at[v], foot_ref.at[v], sems.at[v])

    @pl.when(view == 0)
    def _():
        for v in range(foot_ref.shape[0]):
            fetch(v).start()
        ext_ref[...] = jnp.zeros_like(ext_ref)
        ext_ref[:slices] = act_ref[...]
        ext_ref[slices : slices + margin] = above_ref[...]
        ext_ref[slices + margin : slices + 2 * margin] = below_ref[...]
        rows_ref[...] = jnp.dot(
            op_ref[...], ext_ref[...], preferred_element_type=f32, precision=lax.Precision.HIGHEST
        ).astype(bf16)

    fetch(view).wait()
    projected = jnp.dot(rows_ref[...], foot_ref[view], preferred_element_type=f32) * (1.0 / pixels)
    for lane in range(lanes):
        flat = rand_refs[lane].reshape(segs * slices, LANES)
        order_ref = order_refs[lane]
        for g in range(segs):
            for a in range(inner):
                got = flat[pl.ds(g * slices + a, count, stride=inner), :].astype(f32)
                order_ref[pl.ds(g * inner + a, count, stride=segs * inner), :] = 0.25 * (got + 1.0)
        cols = slice(lane * LANES, (lane + 1) * LANES)
        eff = eff_ref[0, :, cols]
        value = eff / (eff * projected[:, cols] + order_ref[...])
        o_ref[0, :, :, :, cols] = value.reshape(*o_ref.shape[1:4], LANES)


def forward(operator, activity, above, below, footprint, randoms, efficiency):
    segs, views, slices, bins = randoms.shape
    pixels = footprint.shape[1]
    rows = segs * slices
    inner = 2 * segs
    lanes = [
        pl.BlockSpec((segs, 1, slices, LANES), lambda v, lane=lane: (0, v, 0, lane))
        for lane in range(lane_blocks(bins))
    ]
    return pl.pallas_call(
        forward_kernel,
        grid=(views,),
        in_specs=[
            VMEM,
            VMEM,
            VMEM,
            VMEM,
            HBM,
            pl.BlockSpec((1, 1, bins), lambda v: (v, 0, 0)),
        ]
        + lanes,
        out_specs=pl.BlockSpec((1, 2, rows // inner // 2, inner, bins), lambda v: (v, 0, 0, 0, 0)),
        out_shape=pltpu.HBM((views, 2, rows // inner // 2, inner, bins), f32),
        scratch_shapes=[pltpu.VMEM(footprint.shape, footprint.dtype), pltpu.VMEM((rows, pixels), bf16)]
        + [pltpu.VMEM((rows, LANES), f32)] * len(lanes)
        + [pltpu.VMEM((operator.shape[1], pixels), f32), pltpu.SemaphoreType.DMA((views,))],
        compiler_params=params(40),
        cost_estimate=SMALL,
    )(operator, activity, above, below, footprint, efficiency, *[randoms] * len(lanes))


def back_project(operator, weighted, foot):
    ext = operator.shape[0]
    hi, lo = split_two(operator)
    both = jnp.dot(jnp.concatenate([hi, lo], axis=0), weighted, preferred_element_type=f32)
    hi, lo = split_two(both[:ext] + both[ext:])
    spread = lax.dot_general(
        jnp.concatenate([hi, lo], axis=0), foot, (((1,), (1,)), ((), ())), preferred_element_type=f32
    )
    return spread[:ext] + spread[ext:]


def ratio(factor, rows_in):
    scaled = factor * rows_in
    return scaled.reshape(-1, scaled.shape[-1]).astype(bf16)


def start_all(copies):
    for copy in copies:
        copy.start()


def back_staged_kernel(
    edge,
    half_ref,
    op_ref,
    staged_hbm,
    part_ref,
    factor_hbm,
    foot_hbm,
    acc_ref,
    own_ref,
    factor_ref,
    foot_ref,
    sems,
):
    half = half_ref[0]
    views, _, count, inner, bins = factor_ref.shape
    bare = views - own_ref.shape[0]
    firsts = factor_hbm.shape[0] - views
    middles = (part_ref.shape[0] - 2 * edge * views) // (count - 2 * edge)

    def copies(v):
        own = []
        if v >= bare:
            slot = bare + 2 * (v - bare)
            own = [pltpu.make_async_copy(staged_hbm.at[:, slot], own_ref.at[v - bare], sems.at[v, 0])]
        return own + [
            pltpu.make_async_copy(factor_hbm.at[firsts + v], factor_ref.at[v], sems.at[v, 1]),
            pltpu.make_async_copy(foot_hbm.at[firsts + v], foot_ref.at[v], sems.at[v, 2]),
        ]

    for v in range(views):
        start_all(copies(v))
    operator = jnp.concatenate([op_ref[half], op_ref[1 - half]], axis=1)
    for v in range(views):
        for copy in copies(v):
            copy.wait()
        far = factor_ref[v, 1 - half]
        if v >= bare:
            own = ratio(factor_ref[v, half], own_ref[v - bare])
        else:
            own = jnp.zeros((count * inner, bins), bf16)
        low = ratio(far[:edge], part_ref[2 * edge * v : 2 * edge * v + edge])
        high = ratio(far[count - edge :], part_ref[2 * edge * v + edge : 2 * edge * (v + 1)])
        if v < middles:
            first = 2 * edge * views + (count - 2 * edge) * v
            middle = ratio(far[edge : count - edge], part_ref[first : first + count - 2 * edge])
        else:
            middle = jnp.zeros(((count - 2 * edge) * inner, bins), bf16)
        spread = back_project(operator, jnp.concatenate([own, low, middle, high], axis=0), foot_ref[v])
        if v == 0:
            acc_ref[...] = spread
        else:
            acc_ref[...] += spread


def back_staged(half, operator, staged, part, factor, footprint, edge, views):
    ext = operator.shape[1]
    count, slots, inner, bins = staged.shape
    pixels = footprint.shape[1]
    return pl.pallas_call(
        functools.partial(back_staged_kernel, edge),
        in_specs=[SMEM, VMEM, HBM, VMEM, HBM, HBM],
        out_specs=VMEM,
        out_shape=pltpu.VMEM((ext, pixels), f32),
        scratch_shapes=[
            pltpu.VMEM((slots - views, count, inner, bins), f32),
            pltpu.VMEM((views, 2, count, inner, bins), f32),
            pltpu.VMEM((views, pixels, bins), bf16),
            pltpu.SemaphoreType.DMA((views, 3)),
        ],
        compiler_params=params(52),
        cost_estimate=LARGE,
    )(half, operator, staged, part, factor, footprint)


def back_near_kernel(
    half_ref, me_ref, op_ref, near_hbm, factor_hbm, foot_hbm, in_ref, acc_ref, keep_ref, give_ref, *scratch
):
    near_ref, factor_ref, foot_ref, sum_ref, sems = scratch
    half = half_ref[0]
    views = factor_ref.shape[0]
    firsts = near_hbm.shape[1] - views

    def copies(v):
        slot, size = (2 * v, 2) if v < firsts else (firsts + v, 1)
        return [
            pltpu.make_async_copy(
                near_hbm.at[:, pl.ds(slot, size)], near_ref.at[:, pl.ds(slot, size)], sems.at[v, 0]
            ),
            pltpu.make_async_copy(factor_hbm.at[v], factor_ref.at[v], sems.at[v, 1]),
            pltpu.make_async_copy(foot_hbm.at[v], foot_ref.at[v], sems.at[v, 2]),
        ]

    for v in range(views):
        start_all(copies(v))
    operator = jnp.concatenate([op_ref[half], op_ref[1 - half]], axis=1)
    sum_ref[...] = in_ref[...]
    for v in range(views):
        for copy in copies(v):
            copy.wait()
        if v < firsts:
            own = ratio(factor_ref[v, half], near_ref[:, 2 * v])
            far = ratio(factor_ref[v, 1 - half], near_ref[:, 2 * v + 1])
        else:
            own = ratio(factor_ref[v, half], near_ref[:, firsts + v])
            far = jnp.zeros_like(own)
        sum_ref[...] += back_project(operator, jnp.concatenate([own, far], axis=0), foot_ref[v])
    slices, pixels = acc_ref.shape
    margin, width = keep_ref.shape[2:]
    acc_ref[...] = sum_ref[:slices]
    core = me_ref[0] % 2
    for k in range(4):
        for c in range(2):
            block = me_ref[0] ^ (2 * k + c)
            cols = pl.ds(pl.multiple_of(block * width, width), width)
            pair = sum_ref[slices : slices + 2 * margin, cols] * (1.0 / pixels)
            up, down = pair[:margin], pair[margin:]
            keep_ref[c, k] = jnp.where(core == 0, down, up)
            give_ref[c, k] = jnp.where(core == 0, up, down)


def back_near(half, me, operator, near, factor, footprint, acc, slices, margin, views):
    count, slots, inner, bins = near.shape
    pixels = footprint.shape[1]
    halo = jax.ShapeDtypeStruct((2, 4, margin, pixels // 8), f32)
    return pl.pallas_call(
        back_near_kernel,
        in_specs=[SMEM, SMEM, VMEM, HBM, HBM, HBM, VMEM],
        out_specs=[VMEM] * 3,
        out_shape=[jax.ShapeDtypeStruct((slices, pixels), f32), halo, halo],
        scratch_shapes=[
            pltpu.VMEM((count, slots, inner, bins), f32),
            pltpu.VMEM((views, 2, count, inner, bins), f32),
            pltpu.VMEM((views, pixels, bins), bf16),
            pltpu.VMEM(acc.shape, f32),
            pltpu.SemaphoreType.DMA((views, 3)),
        ],
        compiler_params=params(52),
        cost_estimate=SMALL,
    )(half, me, operator, near, factor, footprint, acc)


def far_slot(v, views, slots):
    bare = 2 * views - slots
    return v if v < bare else bare + 2 * (v - bare) + 1


def part_kernel(edge, views, staged_hbm, part_ref, sems):
    count, slots = staged_hbm.shape[:2]
    middle = count - 2 * edge
    copies = []

    def add(first, size, v, place):
        copies.append(
            pltpu.make_async_copy(
                staged_hbm.at[pl.ds(first, size), far_slot(v, views, slots)],
                part_ref.at[pl.ds(place, size)],
                sems.at[len(copies)],
            )
        )

    for v in range(views):
        add(0, edge, v, 2 * edge * v)
        add(count - edge, edge, v, 2 * edge * v + edge)
    for v in range((part_ref.shape[0] - 2 * edge * views) // middle):
        add(edge, middle, v, 2 * edge * views + middle * v)
    start_all(copies)
    for copy in copies:
        copy.wait()


def part_of(staged, edge, views, lasts):
    count, slots, inner, bins = staged.shape
    part = 2 * edge * views + (count - 2 * edge) * (views - lasts)
    return pl.pallas_call(
        functools.partial(part_kernel, edge, views),
        in_specs=[HBM],
        out_specs=VMEM,
        out_shape=pltpu.VMEM((part, inner, bins), f32),
        scratch_shapes=[pltpu.SemaphoreType.DMA((3 * views,))],
        compiler_params=params(16),
        cost_estimate=SMALL,
    )(staged)


def last_kernel(edge, views, staged_hbm, _, last_ref, sems):
    slots = staged_hbm.shape[1]
    middle, lasts = last_ref.shape[:2]
    copies = [
        pltpu.make_async_copy(
            staged_hbm.at[pl.ds(edge, middle), far_slot(views - lasts + v, views, slots)],
            last_ref.at[:, v],
            sems.at[v],
        )
        for v in range(lasts)
    ]
    start_all(copies)
    for copy in copies:
        copy.wait()


def last_of(staged, edge, views, lasts, after):
    count, _, inner, bins = staged.shape
    return pl.pallas_call(
        functools.partial(last_kernel, edge, views),
        in_specs=[HBM, pl.BlockSpec(memory_space=pl.ANY)],
        out_specs=VMEM,
        out_shape=pltpu.VMEM((count - 2 * edge, lasts, inner, bins), f32),
        scratch_shapes=[pltpu.SemaphoreType.DMA((lasts,))],
        compiler_params=params(16),
        cost_estimate=SMALL,
    )(staged, after)


def crossing_kernel(half_ref, m_hbm, o_ref, sem):
    views, count = o_ref.shape[1], o_ref.shape[3]
    first = pl.multiple_of((1 - half_ref[0]) * count, count)
    copy = pltpu.make_async_copy(m_hbm.at[:, pl.ds(0, views), :, pl.ds(first, count)], o_ref, sem)
    copy.start()
    copy.wait()


def crossing(half, measured, views):
    segs, _, inner, slabs, bins = measured.shape
    return pl.pallas_call(
        crossing_kernel,
        in_specs=[SMEM, HBM],
        out_specs=VMEM,
        out_shape=pltpu.VMEM((segs, views, inner, slabs // 2, bins), f32),
        scratch_shapes=[pltpu.SemaphoreType.DMA],
        compiler_params=params(52),
        cost_estimate=SMALL,
    )(half, measured)


def mark_kernel(x_ref, o_ref):
    o_ref[...] = jnp.zeros_like(o_ref)


def mark(x):
    return pl.pallas_call(
        mark_kernel,
        in_specs=[pl.BlockSpec(memory_space=pl.ANY)],
        out_specs=VMEM,
        out_shape=jax.ShapeDtypeStruct((8, LANES), f32),
        compiler_params=params(16),
        cost_estimate=LARGE,
    )(x)


def fetch_kernel(half_ref, factor_hbm, foot_hbm, _, factor_ref, foot_ref, sems):
    views = foot_ref.shape[0]
    first = foot_hbm.shape[0] - views
    far = 1 - half_ref[0]
    copies = [
        pltpu.make_async_copy(factor_hbm.at[pl.ds(first, views), far], factor_ref, sems.at[views])
    ] + [pltpu.make_async_copy(foot_hbm.at[first + v], foot_ref.at[v], sems.at[v]) for v in range(views)]
    start_all(copies)
    for copy in copies:
        copy.wait()


def fetch_last(half, factor, footprint, after, views):
    return pl.pallas_call(
        fetch_kernel,
        in_specs=[SMEM, HBM, HBM, pl.BlockSpec(memory_space=pl.ANY)],
        out_specs=[VMEM] * 2,
        out_shape=[
            pltpu.VMEM((views,) + factor.shape[2:], f32),
            pltpu.VMEM((views,) + footprint.shape[1:], footprint.dtype),
        ],
        scratch_shapes=[pltpu.SemaphoreType.DMA((views + 1,))],
        compiler_params=params(45),
        cost_estimate=SMALL,
    )(half, factor, footprint, after)


def back_last_kernel(half_ref, me_ref, op_ref, x_ref, factor_ref, foot_ref, in_ref, *refs):
    mine_refs, (other_ref, acc_ref) = refs[:4], refs[4:]
    slices, pixels = acc_ref.shape
    middle, views, inner, bins = x_ref.shape
    count = factor_ref.shape[1]
    edge = (count - middle) // 2
    far = 1 - half_ref[0]
    gap = jnp.zeros((edge * inner, bins), bf16)
    operator = op_ref[far, :slices]
    acc_ref[...] = in_ref[...]
    for v in range(views):
        weighted = ratio(factor_ref[v, edge : count - edge], x_ref[:, v])
        acc_ref[...] += back_project(operator, jnp.concatenate([gap, weighted, gap], axis=0), foot_ref[v])
    width = mine_refs[0].shape[1]
    for k in range(4):
        for c in range(2):
            block = me_ref[0] ^ (2 * k + c)
            part = acc_ref[:, pl.ds(pl.multiple_of(block * width, width), width)] * (1.0 / pixels)
            if c == 0:
                mine_refs[k][...] = part
            else:
                other_ref[k] = part


def back_last(half, me, operator, rows_in, factor, footprint, acc):
    slices, pixels = acc.shape
    width = pixels // 8
    return pl.pallas_call(
        back_last_kernel,
        in_specs=[SMEM, SMEM] + [VMEM] * 5,
        out_specs=[VMEM] * 5,
        out_shape=[pltpu.VMEM((slices, width), f32)] * 4 + [pltpu.VMEM((4, slices, width), f32)],
        scratch_shapes=[pltpu.VMEM((slices, pixels), f32)],
        compiler_params=params(24),
        cost_estimate=SMALL,
    )(half, me, operator, rows_in, factor, footprint, acc)


def pair_kernel(me_ref, flip_ref, *refs):
    mine_refs, theirs_ref, halo_ref, across_ref, out_refs = refs[:4], refs[4], refs[5], refs[6], refs[7:]
    core = me_ref[0] % 2
    slices, _ = mine_refs[0].shape
    margin = halo_ref.shape[2]
    for k in range(4):
        here, there = halo_ref[0, k ^ flip_ref[0]], across_ref[k ^ flip_ref[1]]
        above = jnp.where(core == 0, here, there)
        below = jnp.where(core == 0, there, here)
        out_refs[k][...] = mine_refs[k][...] + theirs_ref[k]
        out_refs[k][:margin] += above
        out_refs[k][slices - margin :] += below


def pair_sum(me, flip, mine, theirs, halo, across):
    return pl.pallas_call(
        pair_kernel,
        in_specs=[SMEM] * 2 + [VMEM] * 7,
        out_specs=[VMEM] * 4,
        out_shape=[pltpu.VMEM(x.shape, f32) for x in mine],
        compiler_params=params(16),
        cost_estimate=SMALL,
    )(me, flip, *mine, theirs, halo, across)


def assemble_kernel(me_ref, *refs):
    near_refs, far_ref, o_ref = refs[:4], refs[4], refs[5]
    width = near_refs[0].shape[1]
    for k in range(4):
        for c in range(2):
            block = me_ref[0] ^ (2 * k + c)
            part = near_refs[k][...] if c == 0 else far_ref[k]
            o_ref[:, pl.ds(pl.multiple_of(block * width, width), width)] = part


def assemble(me, near, far):
    slices, width = near[0].shape
    return pl.pallas_call(
        assemble_kernel,
        in_specs=[SMEM] + [VMEM] * 5,
        out_specs=VMEM,
        out_shape=jax.ShapeDtypeStruct((slices, width * 8), f32),
        compiler_params=params(16),
    )(me, *near, far)


def local(activity, measured, randoms, footprint, kernel, dead_counts, crystals, sensitivity):
    segs, views, inner, slabs, bins = measured.shape
    slices, pixels = activity.shape
    taps = kernel.shape[1]
    margin = (taps - 1) // 2
    width = pixels // 8
    group = lax.axis_index("seg")
    me = group.astype(jnp.int32).reshape(1)
    halves = lax.axis_size("seg") // 2

    def swap(x, k):
        return lax.ppermute(x, "seg", [(i, i ^ k) for i in range(2 * halves)])

    def shift(x, ups):
        pairs = []
        for j in range(2 * halves):
            for i in range(slabs - 1):
                source, target = (i + 1, i) if j % 2 in ups else (i, i + 1)
                to = j ^ MIRROR if i + 1 == slabs // 2 else j
                pairs.append((j * slabs + source, to * slabs + target))
        return lax.ppermute(x, ("seg", "slab"), pairs)

    count = slabs // 2
    slab = lax.axis_index("slab").astype(jnp.int32)
    half = (slab // count).reshape(1)
    edge = margin // inner
    firsts, bare, lasts = 3, 2, LASTS
    behind = views - firsts

    def cross(x):
        return lax.ppermute(x, "slab", [(i, (i + count) % slabs) for i in range(slabs)])

    def exchange(x):
        groups = [[h * count + i for i in range(count)] for h in range(2)]
        return lax.all_to_all(x, "slab", split_axis=0, concat_axis=0, tiled=True, axis_index_groups=groups)

    ext = slices + 2 * margin
    early = cross(crossing(half, measured, firsts))
    staged = relay(half, measured, (1,), firsts, bare, count, 2 * behind - bare)
    staged = relay(
        half, measured, (0, 1), firsts + bare, behind - bare, count, 2 * behind - bare, into=staged, slot=bare // 2
    )
    staged, near_activity = lax.optimization_barrier((staged, activity))
    staged = exchange(staged)
    near = relay(half, measured, (0,), 0, firsts, count, 2 * firsts + bare, step=2)
    near = relay(half, measured, (0,), firsts, bare, count, 2 * firsts + bare, into=near, slot=2 * firsts)
    efficiency, operator, operator_t = setup(me, kernel, dead_counts, crystals, slices, segs, inner, halves)
    even = group % 2 == 0
    above = shift(near_activity[slices - margin :], ())
    below = shift(near_activity[:margin], (0, 1))
    staged, near, begun, efficiency, operator, operator_t, above, below = lax.optimization_barrier(
        (staged, near, mark(early), efficiency, operator, operator_t, above, below)
    )
    part = cross(part_of(staged, edge, behind, lasts))
    near = relay(
        half, early, (1,), 0, firsts, count, 2 * firsts + bare, into=near, slot=1, step=2, after=[begun]
    )
    rows_last = cross(last_of(staged, edge, behind, lasts, near))
    near = exchange(near)
    factor = forward(operator, activity, above, below, footprint, randoms, efficiency)

    acc = back_staged(half, operator_t, staged, part, factor, footprint, edge, behind)
    acc, keep, give = back_near(half, me, operator_t, near, factor, footprint, acc, slices, margin, firsts + bare)
    joined = keep + swap(give, 1)[::-1]
    halo = shift(joined, (1,))
    last_factor, last_foot = fetch_last(half, factor, footprint, joined, lasts)
    across = swap(halo[1], 1)
    *mine, other = back_last(half, me, operator_t, rows_last, last_factor, last_foot, acc)
    sides = [jnp.where(even, slab == count, slab == count - 1), jnp.where(even, slab == count - 1, slab == count)]
    flip = jnp.where(jnp.stack(sides), MIRROR // 2, 0).astype(jnp.int32)
    pair = pair_sum(me, flip, mine, swap(other, 1), halo, across)
    total = pair[0]
    for k in range(1, 4):
        total = total + swap(pair[k], 2 * k)
    start = group * width
    gain = lax.dynamic_slice_in_dim(activity, start, width, 1) / lax.dynamic_slice_in_dim(
        sensitivity, start, width, 1
    )
    block = total * gain
    near = [block] + [swap(block, 2 * k) for k in range(1, 4)]
    far = swap(jnp.stack(near), 1)
    return assemble(me, near, far)


def solution(mesh):
    placed = (
        P("slab", None),
        P("seg", None, "slab", None, None),
        P("seg", None, "slab", None),
        P(),
        P(),
        P(),
        P(),
        P("slab", None),
    )
    return jax.shard_map(
        local, mesh=mesh, in_specs=placed, out_specs=P("slab", None), check_vma=False
    )
```
